32 devices in a mesh: dp: 16 (over z, x, core), tensor: 2 (over y).
Axes of the slice: x: 2, y: 2, z: 4, core: 2. Of those that a mesh axis runs over, the one named last changes fastest.
Arguments:
- tokens: bfloat16 [2, 2048, 2048], P(None, 'dp', 'tensor'), may hold values from -6 to 6
- segments: int32 [2, 2048], P(None, 'dp'), may hold values from 0 to 1, as said below
- cotangent: bfloat16 [2, 2048, 2048], P(None, 'dp', 'tensor'), may hold values from -6 to 6
- norm_gain: bfloat16 [2048], P('dp'), may hold values from 0.5 to 1.5
- w_in: bfloat16 [2048, 2, 4096], P('dp', None, 'tensor'), may hold values from -0.125 to 0.125
- conv_w: bfloat16 [4, 4096], P(None, ('tensor', 'dp')), may hold values from -3 to 3
- conv_b: bfloat16 [4096], P(('tensor', 'dp')), may hold values from -1.5 to 1.5
- w_x: bfloat16 [4096, 160], P(('tensor', 'dp')), may hold values from -0.375 to 0.375
- w_dt: bfloat16 [128, 4096], P('dp', 'tensor'), may hold values from -0.5 to 0.5
- dt_bias: bfloat16 [4096], P(('tensor', 'dp')), may hold values from -7 to -2
- a_log: bfloat16 [4096, 16], P(('tensor', 'dp')), may hold values from -4 to 2.796875
- d_skip: bfloat16 [4096], P(('tensor', 'dp')), may hold values from 0.19921875 to 3.5
- w_out: bfloat16 [4096, 2048], P('tensor', 'dp'), may hold values from -0.1875 to 0.1875
Outputs:
- block_out: bfloat16 [2, 2048, 2048], P(None, 'dp', 'tensor')
- input_grad: float32 [2, 2048, 2048], P(None, 'dp', 'tensor')
- grad_gain: float32 [2048], P('dp')
- grad_w_in: float32 [2048, 2, 4096], P('dp', None, 'tensor')
- grad_conv_w: float32 [4, 4096], P(None, ('tensor', 'dp'))
- grad_conv_b: float32 [4096], P(('tensor', 'dp'))
- grad_w_x: float32 [4096, 160], P(('tensor', 'dp'))
- grad_w_dt: float32 [128, 4096], P('dp', 'tensor')
- grad_dt_bias: float32 [4096], P(('tensor', 'dp'))
- grad_a_log: float32 [4096, 16], P(('tensor', 'dp'))
- grad_skip: float32 [4096], P(('tensor', 'dp'))
- grad_w_out: float32 [4096, 2048], P('tensor', 'dp')
The draws below stay inside these ranges and needn't reach their ends.
Inputs may be any that keep to these rules, and one draw needn't show every extreme that they name: `segments`: in each sequence the mark is 0 at the first token and switches between 0 and 1 exactly where a new document starts; documents hold 200 to 2000 tokens except the last of a sequence, which may be shorter; one sequence, drawn from the seed, is a single document.
All inputs are finite; a program needn't handle non-finite values.
Results may differ from the reference program's by a relative error of at most 0.007.
The reference program's roundings to bfloat16 on the way count: a program that leaves them out, or rounds other values in their place, can miss the bound.
Values may be sent and summed in bfloat16 or wider, within the bound.
No kernel may reach another device: no remote copies, remote signals or barrier semaphores. Data moves between devices by JAX's collectives and lax.ppermute only.
A program may use at most 192 MiB of HBM per device.

```python
import jax
import jax.numpy as jnp
from jax import lax

D = 2048
INNER = 4096
NSTATE = 16
RANK = 128
CONV = 4
MB = 2
DOC_MIN = 200
DOC_MAX = 2000
LENGTH = 2048


def draw_segments(key, part):
    key = jax.random.fold_in(key, 7)
    key_lengths, key_pick = jax.random.split(key)
    doc_count = LENGTH // DOC_MIN + 2
    doc_lengths = jax.random.randint(key_lengths, (MB, doc_count), DOC_MIN, DOC_MAX + 1)
    doc_ends = jnp.cumsum(doc_lengths, axis=1)
    places = jnp.arange(LENGTH, dtype=jnp.int32)
    numbers = jnp.sum((doc_ends[:, None, :] <= places[None, :, None]).astype(jnp.int32), axis=2)
    single = jax.random.randint(key_pick, (), 0, MB)
    sequence_ids = jnp.arange(MB, dtype=jnp.int32)
    return jnp.where((sequence_ids == single)[:, None], 0, numbers % 2).astype(jnp.int32)


def level_of(stream_key, shape, cuts, least, largest):
    gain = 1.0
    for position, shards_of in cuts:
        draws = jax.random.uniform(jax.random.fold_in(jax.random.fold_in(stream_key, 6), position), (shards_of,), jnp.float32, least / len(cuts), largest / len(cuts))
        gain = gain * jnp.repeat(jnp.exp(draws), shape[position] // shards_of).reshape((-1,) + (1,) * (len(shape) - 1 - position))
    return gain


def gaussian(stream_key, extent, width, bound, cuts=(), kind=jnp.bfloat16):
    loudness = level_of(stream_key, extent, cuts, -0.22, 0.18) if cuts else 1.0
    values = jax.random.normal(stream_key, extent, jnp.float32) * width * loudness
    return jnp.minimum(jnp.maximum(values, -bound), bound).astype(kind)


def setup_inputs(seed: int = 0) -> dict:
    streams_of = jax.random.split(jax.random.key(seed), 14)
    tokens = gaussian(streams_of[0], (MB, LENGTH, D), 1.0, 6.0, ((1, 16), (2, 2)))
    segments = draw_segments(jax.random.fold_in(streams_of[13], 71), 0)
    cotangent = gaussian(streams_of[2], (MB, LENGTH, D), 1.0, 6.0, ((1, 16), (2, 2)))
    norm_gain = jnp.clip(1.0 + 0.1 * jax.random.normal(streams_of[3], (D,), jnp.float32), 0.5, 1.5).astype(jnp.bfloat16)
    w_in = gaussian(streams_of[4], (D, 2, INNER), D ** -0.5, 0.125, ((0, 16), (2, 2)))
    conv_w = gaussian(streams_of[5], (CONV, INNER), CONV ** -0.5, 3.0, ((1, 32),))
    conv_b = gaussian(streams_of[6], (INNER,), 0.3, 1.5, ((0, 32),))
    w_x = gaussian(streams_of[7], (INNER, RANK + 2 * NSTATE), (INNER // 16) ** -0.5, 0.375, ((0, 32),))
    w_dt = gaussian(streams_of[8], (RANK, INNER), RANK ** -0.5, 0.5, ((0, 16), (1, 2)))
    dt_bias = jnp.clip(-7.0 + 5.0 * jax.random.uniform(streams_of[9], (INNER,), jnp.float32) ** level_of(streams_of[9], (INNER,), ((0, 32),), -0.2, 0.2), -7.0, -2.0).astype(jnp.bfloat16)
    a_log = jnp.clip(-4.0 + 6.796875 * jax.random.uniform(streams_of[10], (INNER, NSTATE), jnp.float32) ** level_of(streams_of[10], (INNER, NSTATE), ((0, 32),), -0.2, 0.2), -4.0, 2.796875).astype(jnp.bfloat16)
    d_skip = jnp.clip(0.19921875 + 3.3007812 * jax.random.uniform(streams_of[11], (INNER,), jnp.float32) ** level_of(streams_of[11], (INNER,), ((0, 32),), -0.2, 0.2), 0.19921875, 3.5).astype(jnp.bfloat16)
    w_out = gaussian(streams_of[12], (INNER, D), (INNER // 4) ** -0.5, 0.1875, ((0, 2), (1, 16)))
    return {"tokens": tokens, "segments": segments, "cotangent": cotangent, "norm_gain": norm_gain, "w_in": w_in, "conv_w": conv_w, "conv_b": conv_b, "w_x": w_x, "w_dt": w_dt, "dt_bias": dt_bias, "a_log": a_log, "d_skip": d_skip, "w_out": w_out}


@jax.custom_vjp
def low(v):
    return lax.optimization_barrier(v.astype(jnp.bfloat16)).astype(jnp.float32)

@jax.custom_vjp
def low_back(v):
    return v

def low_keep(v):
    return (low(v), None)

def low_pass(kept, grad):
    return (grad,)

def back_keep(v):
    return (v, None)

def back_low(kept, grad):
    return (low(grad),)
low.defvjp(low_keep, low_pass)
low_back.defvjp(back_keep, back_low)
epsilon = 1e-05
scan_rows = 64

def matmul(left, right):
    return jnp.dot(left, right, precision=lax.Precision.HIGHEST, preferred_element_type=jnp.float32)

def selective(delta, conv_out, b_part, c_part, keep_rows, a_mat):
    block_count = delta.shape[0] // scan_rows

    def run_block(state_now, pieces):

        def token_step(carried, token_row):
            delta_row, conv_row, b_row, c_row, keep_row = token_row
            decay_row = jnp.exp(delta_row[:, None] * a_mat) * keep_row
            carried = decay_row * carried + (delta_row * conv_row)[:, None] * b_row[None, :]
            return (carried, lax.optimization_barrier(jnp.sum(carried * c_row[None, :], axis=1)))
        return lax.scan(token_step, state_now, pieces)
    pieces = tuple((member.reshape((block_count, scan_rows) + member.shape[1:]) for member in (delta, conv_out, b_part, c_part, keep_rows)))
    start_state = jnp.zeros(a_mat.shape, jnp.float32)
    final_state, outputs = lax.scan(jax.checkpoint(run_block), start_state, pieces)
    return outputs.reshape(delta.shape)

def forward(tokens, params, segments):
    norm_gain, w_in, conv_w, conv_b, w_x, w_dt, dt_bias, a_log, d_skip, w_out = params
    seq_rows = tokens.shape[0]
    scale_rows = lax.rsqrt(lax.optimization_barrier(jnp.mean(tokens * tokens, axis=1, keepdims=True)) + epsilon)
    normed = low(tokens * scale_rows * norm_gain)
    both_parts = low_back(matmul(normed, w_in.reshape(D, 2 * INNER))).reshape(seq_rows, 2, INNER)
    inner_rows = low(both_parts[:, 0])
    gate_rows = both_parts[:, 1]
    marks_all = jnp.concatenate([jnp.full((CONV - 1,), -1, jnp.int32), segments.astype(jnp.int32)])
    padded = jnp.concatenate([jnp.zeros((CONV - 1, INNER), jnp.float32), inner_rows], axis=0)
    mixed_rows = jnp.zeros((seq_rows, INNER), jnp.float32) + conv_b
    for offset in range(CONV):
        same_doc = (marks_all[offset:offset + seq_rows] == segments).astype(jnp.float32)
        mixed_rows = mixed_rows + conv_w[offset] * padded[offset:offset + seq_rows] * same_doc[:, None]
    conv_out = low(jax.nn.silu(mixed_rows))
    projected = low_back(matmul(conv_out, w_x))
    rank_part = low(projected[:, :RANK])
    b_part = projected[:, RANK:RANK + NSTATE]
    c_part = projected[:, RANK + NSTATE:]
    pre_delta = low_back(matmul(rank_part, w_dt)) + dt_bias
    delta = jax.nn.softplus(pre_delta)
    keep_rows = (marks_all[CONV - 2:CONV - 2 + seq_rows] == segments).astype(jnp.float32)
    a_mat = -jnp.exp(a_log)
    readout = selective(delta, conv_out, b_part, c_part, keep_rows, a_mat)
    ssm_rows = readout + d_skip * conv_out
    gated = low(ssm_rows * jax.nn.silu(gate_rows))
    return tokens + low_back(matmul(gated, w_out))

def reference(tokens, segments, cotangent, norm_gain, w_in, conv_w, conv_b, w_x, w_dt, dt_bias, a_log, d_skip, w_out):
    weights = tuple((weight_arg.astype(jnp.float32) for weight_arg in (norm_gain, w_in, conv_w, conv_b, w_x, w_dt, dt_bias, a_log, d_skip, w_out)))

    def one_sequence(totals, pieces):
        seq_tokens, seq_marks, seq_cot = pieces
        result, pullback = jax.vjp(lambda values, params: forward(values, params, seq_marks), seq_tokens.astype(jnp.float32), weights)
        grad_values, grad_params = pullback(seq_cot.astype(jnp.float32))
        totals = tuple((total + extra for total, extra in zip(totals, grad_params)))
        return (totals, (result.astype(jnp.bfloat16), grad_values))
    zero_grads = tuple((jnp.zeros(weight_arg.shape, jnp.float32) for weight_arg in weights))
    totals, (outputs, input_grads) = lax.scan(one_sequence, zero_grads, (tokens, segments, cotangent))
    return (outputs, input_grads, totals[0], totals[1], totals[2], totals[3], totals[4], totals[5], totals[6], totals[7], totals[8], totals[9])
```

```python
import functools

import jax
import jax.numpy as jnp
from jax import lax
from jax.experimental import pallas as pl
from jax.experimental.pallas import tpu as pltpu
from jax.sharding import PartitionSpec as P

NSTATE = 16
RANK = 128
LANES = 128
DP = "dp"
TENSOR = "tensor"
GROUP = 8
LOG2E = 1.4426950408889634


def fold(parts, masks):
    width = 1
    while len(parts) > 1:
        joined = []
        for first, second in zip(parts[0::2], parts[1::2]):
            mask = masks[width]
            joined.append(
                jnp.where(mask, first, second) + pltpu.roll(jnp.where(mask, second, first), width, 0)
            )
        parts = joined
        width *= 2
    return parts[0]


def fold_masks():
    row = lax.broadcasted_iota(jnp.int32, (GROUP, LANES), 0)
    return {width: (row & width) == 0 for width in (1, 2, 4)}


def halves(value):
    return value[:GROUP] + value[GROUP:]


def spread(row):
    return jnp.broadcast_to(row, (NSTATE, LANES))


def cols(k):
    return pl.ds(k * LANES, LANES)


def forward_end_kernel(step_ref, flow_ref, b_ref, rate_ref, end_ref):
    groups, unused, width = step_ref.shape
    tiles = width // LANES
    rates = [rate_ref[:, cols(k)] for k in range(tiles)]

    def body(group, states):
        states = list(states)
        for j in range(GROUP):
            t = group * GROUP + j
            b_now = b_ref[t, :NSTATE, :]
            for k in range(tiles):
                decay = jnp.exp2(rates[k] * spread(step_ref[group, j : j + 1, cols(k)]))
                states[k] = decay * states[k] + b_now * spread(flow_ref[group, j : j + 1, cols(k)])
        return tuple(states)

    start = tuple(jnp.zeros((NSTATE, LANES), jnp.float32) for _ in range(tiles))
    ends = lax.fori_loop(0, groups, body, start)
    for k in range(tiles):
        end_ref[:, cols(k)] = ends[k]


def reverse_end_kernel(step_ref, grad_ref, c_ref, rate_ref, end_ref):
    groups, unused, width = step_ref.shape
    tiles = width // LANES
    rates = [rate_ref[:, cols(k)] for k in range(tiles)]

    def body(lap, states):
        states = list(states)
        group = groups - 1 - lap
        for j in reversed(range(GROUP)):
            t = group * GROUP + j
            c_now = c_ref[t, NSTATE:, :]
            for k in range(tiles):
                decay = jnp.exp2(rates[k] * spread(step_ref[group, j : j + 1, cols(k)]))
                states[k] = decay * (states[k] + c_now * spread(grad_ref[group, j : j + 1, cols(k)]))
        return tuple(states)

    start = tuple(jnp.zeros((NSTATE, LANES), jnp.float32) for _ in range(tiles))
    ends = lax.fori_loop(0, groups, body, start)
    for k in range(tiles):
        end_ref[:, cols(k)] = ends[k]


def forward_kernel(step_ref, flow_ref, bc_ref, rate_ref, enter_ref, out_ref):
    groups, unused, width = step_ref.shape
    tiles = width // LANES
    rates = [rate_ref[:, cols(k)] for k in range(tiles)]
    masks = fold_masks()

    def body(group, states):
        states = list(states)
        parts = [[] for _ in range(tiles)]
        for j in range(GROUP):
            t = group * GROUP + j
            b_now, c_now = bc_ref[t, :NSTATE, :], bc_ref[t, NSTATE:, :]
            for k in range(tiles):
                decay = jnp.exp2(rates[k] * spread(step_ref[group, j : j + 1, cols(k)]))
                states[k] = decay * states[k] + b_now * spread(flow_ref[group, j : j + 1, cols(k)])
                parts[k].append(halves(states[k] * c_now))
        for k in range(tiles):
            out_ref[group, :, cols(k)] = fold(parts[k], masks)
        return tuple(states)

    start = tuple(enter_ref[:, cols(k)] for k in range(tiles))
    lax.fori_loop(0, groups, body, start)


def reverse_kernel(
    held,
    step_ref,
    delta_ref,
    flow_ref,
    conv_ref,
    grad_ref,
    bc_ref,
    rate_ref,
    a_ref,
    enter_ref,
    leave_ref,
    *refs,
):
    gdelta_ref, gconv_ref, gbc_ref, ga_ref, decay_scr, state_scr = refs[held:]
    groups, unused, width = step_ref.shape
    tiles = width // LANES
    rates = [rate_ref[:, cols(k)] for k in range(tiles)]
    masks = fold_masks()

    def ahead(group, states):
        states = list(states)
        for j in range(GROUP):
            t = group * GROUP + j
            b_now = bc_ref[t, :NSTATE, :]
            for k in range(tiles):
                decay = jnp.exp2(rates[k] * spread(step_ref[group, j : j + 1, cols(k)]))
                state_scr[t, :, cols(k)] = states[k]
                decay_scr[t, :, cols(k)] = decay
                states[k] = decay * states[k] + b_now * spread(flow_ref[group, j : j + 1, cols(k)])
        return tuple(states)

    start = tuple(enter_ref[:, cols(k)] for k in range(tiles))
    ends = lax.fori_loop(0, groups, ahead, start)
    for k in range(tiles):
        state_scr[groups * GROUP, :, cols(k)] = ends[k]

    @pl.when(pl.program_id(0) == 0)
    def clear():
        gbc_ref[...] = jnp.zeros_like(gbc_ref)

    def back(lap, carried):
        carried, totals = list(carried[0]), list(carried[1])
        group = groups - 1 - lap
        inputs = [[] for _ in range(tiles)]
        drifts = [[] for _ in range(tiles)]
        for j in reversed(range(GROUP)):
            t = group * GROUP + j
            b_now, c_now = bc_ref[t, :NSTATE, :], bc_ref[t, NSTATE:, :]
            sum_b = sum_c = None
            for k in range(tiles):
                grad = spread(grad_ref[group, j : j + 1, cols(k)])
                flow = spread(flow_ref[group, j : j + 1, cols(k)])
                step = spread(delta_ref[group, j : j + 1, cols(k)])
                state_grad = carried[k] + grad * c_now
                inputs[k].insert(0, halves(state_grad * b_now))
                term_b = state_grad * flow
                term_c = state_scr[t + 1, :, cols(k)] * grad
                sum_b = term_b if sum_b is None else sum_b + term_b
                sum_c = term_c if sum_c is None else sum_c + term_c
                carried[k] = decay_scr[t, :, cols(k)] * state_grad
                term = carried[k] * state_scr[t, :, cols(k)]
                drifts[k].insert(0, halves(term * a_ref[:, cols(k)]))
                totals[k] = totals[k] + term * step
            gbc_ref[t, :NSTATE, :] = gbc_ref[t, :NSTATE, :] + sum_b
            gbc_ref[t, NSTATE:, :] = gbc_ref[t, NSTATE:, :] + sum_c
        for k in range(tiles):
            entry = fold(inputs[k], masks)
            gdelta_ref[group, :, cols(k)] = fold(drifts[k], masks) + entry * conv_ref[group, :, cols(k)]
            gconv_ref[group, :, cols(k)] = entry * delta_ref[group, :, cols(k)]
        return (tuple(carried), tuple(totals))

    start = tuple(leave_ref[:, cols(k)] for k in range(tiles))
    zeros = tuple(jnp.zeros((NSTATE, LANES), jnp.float32) for _ in range(tiles))
    unused, totals = lax.fori_loop(0, groups, back, (start, zeros))
    for k in range(tiles):
        ga_ref[:, cols(k)] = totals[k]


def row_spec(rows, width):
    return pl.BlockSpec((None, rows // GROUP, GROUP, width), lambda s, c: (s, 0, 0, c))


def grouped(*arrays):
    return tuple(a.reshape(a.shape[0], -1, GROUP, a.shape[-1]) for a in arrays)


def bc_spec(rows):
    return pl.BlockSpec((None, rows, 2 * NSTATE, LANES), lambda s, c: (s, 0, 0, 0))


def rate_spec(width):
    return pl.BlockSpec((NSTATE, width), lambda s, c: (0, c))


def state_spec(width):
    return pl.BlockSpec((None, NSTATE, width), lambda s, c: (s, 0, c))


def f32(*shape):
    return jax.ShapeDtypeStruct(shape, jnp.float32)


def limits(mb):
    return pltpu.CompilerParams(vmem_limit_bytes=mb * 2**20)


def forward_end(step, flow, bc, rate, width):
    seqs, rows, channels = step.shape
    return pl.pallas_call(
        forward_end_kernel,
        grid=(seqs, channels // width),
        in_specs=[row_spec(rows, width)] * 2 + [bc_spec(rows), rate_spec(width)],
        out_specs=state_spec(width),
        out_shape=f32(seqs, NSTATE, channels),
        compiler_params=limits(40),
        name="forward_end",
    )(*grouped(step, flow), bc, rate)


def reverse_end(step, grad, bc, rate, width):
    seqs, rows, channels = step.shape
    return pl.pallas_call(
        reverse_end_kernel,
        grid=(seqs, channels // width),
        in_specs=[row_spec(rows, width)] * 2 + [bc_spec(rows), rate_spec(width)],
        out_specs=state_spec(width),
        out_shape=f32(seqs, NSTATE, channels),
        compiler_params=limits(40),
        name="reverse_end",
    )(*grouped(step, grad), bc, rate)


def forward_main(step, flow, bc, rate, enter, width):
    seqs, rows, channels = step.shape
    return pl.pallas_call(
        forward_kernel,
        grid=(seqs, channels // width),
        in_specs=[row_spec(rows, width)] * 2 + [bc_spec(rows), rate_spec(width), state_spec(width)],
        out_specs=row_spec(rows, width),
        out_shape=f32(seqs, rows // GROUP, GROUP, channels),
        compiler_params=limits(40),
        name="forward_main",
    )(*grouped(step, flow), bc, rate, enter).reshape(step.shape)


def reverse_main(step, delta, flow, conv, grad, bc, rate, a_mat, enter, leave, width, seq, into=()):
    seqs, rows, channels = step.shape

    def of_seq(*block):
        return pl.BlockSpec((None,) + block, lambda c: (seq,) + (0,) * (len(block) - 1) + (c,))

    row = of_seq(rows // GROUP, GROUP, width)
    state = of_seq(NSTATE, width)
    pairs = pl.BlockSpec((None, rows, 2 * NSTATE, LANES), lambda c: (seq, 0, 0, 0))
    rates = pl.BlockSpec((NSTATE, width), lambda c: (0, c))
    return pl.pallas_call(
        functools.partial(reverse_kernel, len(into)),
        grid=(channels // width,),
        in_specs=[row] * 5
        + [pairs, rates, rates, state, state]
        + [pl.BlockSpec(memory_space=pl.ANY)] * len(into),
        out_specs=[row, row, pairs, state],
        out_shape=[f32(seqs, rows // GROUP, GROUP, channels)] * 2
        + [f32(seqs, rows, 2 * NSTATE, LANES), f32(seqs, NSTATE, channels)],
        input_output_aliases={10 + n: n for n in range(len(into))},
        scratch_shapes=[
            pltpu.VMEM((rows, NSTATE, width), jnp.float32),
            pltpu.VMEM((rows + 1, NSTATE, width), jnp.float32),
        ],
        compiler_params=limits(56),
        name="reverse_main",
    )(*grouped(step, delta, flow, conv, grad), bc, rate, a_mat, enter, leave, *into)


def place_of(piece):
    width = LANES
    return pl.ds(pl.multiple_of((lax.axis_index(DP) ^ piece) * width, width), width)


def piece_spec(n, width, piece=0):
    if n is None:
        return pl.BlockSpec((LANES, width), lambda j: (lax.axis_index(DP) ^ piece, j))
    return pl.BlockSpec((LANES, width), lambda j: (n, j))


def up_kernel(x_ref, *refs):
    pieces, out_ref, x_scr = refs[:-2], refs[-2], refs[-1]

    @pl.when(pl.program_id(0) == 0)
    def order():
        for p in range(len(pieces)):
            x_scr[:, cols(p)] = x_ref[:, place_of(p)]

    weights = jnp.concatenate([ref[...] for ref in pieces], axis=0)
    out_ref[...] = jnp.dot(x_scr[...], weights, preferred_element_type=jnp.float32).astype(
        out_ref.dtype
    )


def up(x, pieces, kind, width=512):
    rows, features = x.shape
    channels = pieces[0][0].shape[1]
    return pl.pallas_call(
        up_kernel,
        grid=(channels // width,),
        in_specs=[pl.BlockSpec((rows, features), lambda j: (0, 0))]
        + [piece_spec(n, width) for unused, n in pieces],
        out_specs=pl.BlockSpec((rows, width), lambda j: (0, j)),
        out_shape=jax.ShapeDtypeStruct((rows, channels), kind),
        scratch_shapes=[pltpu.VMEM((rows, features), x.dtype)],
        compiler_params=limits(40),
        name="up",
    )(x, *[array for array, unused in pieces])


def down_kernel(groups, *refs):
    inputs, pieces = refs[:groups], refs[groups:-3]
    own_ref, other_ref, total = refs[-3:]
    count = len(pieces) // groups
    new = None
    for g, y_ref in enumerate(inputs):
        weights = jnp.concatenate([ref[...] for ref in pieces[g * count : (g + 1) * count]], axis=0)
        term = lax.dot_general(
            y_ref[...], weights, (((1,), (1,)), ((), ())), preferred_element_type=jnp.float32
        )
        new = term if new is None else new + term

    @pl.when(pl.program_id(0) == 0)
    def first():
        total[...] = new

    @pl.when(pl.program_id(0) > 0)
    def later():
        total[...] += new

    @pl.when(pl.program_id(0) == pl.num_programs(0) - 1)
    def last():
        half = count // 2
        mine = lax.axis_index(TENSOR) * half
        for r in range(half):
            own_ref[:, cols(r)] = total[:, place_of(mine + r)]
            other_ref[:, cols(r)] = total[:, place_of((half - mine) + r)].astype(other_ref.dtype)


def down(pairs, kind, width=512):
    rows, channels = pairs[0][0].shape
    count = len(pairs[0][1])
    features = count * LANES
    half = pl.BlockSpec((rows, features // 2), lambda j: (0, 0))
    return pl.pallas_call(
        functools.partial(down_kernel, len(pairs)),
        grid=(channels // width,),
        in_specs=[pl.BlockSpec((rows, width), lambda j: (0, j))] * len(pairs)
        + [
            piece_spec(n, width, piece)
            for unused, pieces in pairs
            for piece, (array, n) in enumerate(pieces)
        ],
        out_specs=[half, half],
        out_shape=[
            jax.ShapeDtypeStruct((rows, features // 2), jnp.float32),
            jax.ShapeDtypeStruct((rows, features // 2), kind),
        ],
        scratch_shapes=[pltpu.VMEM((rows, features), jnp.float32)],
        compiler_params=limits(48),
        name="down",
    )(*[y for y, unused in pairs], *[array for unused, pieces in pairs for array, n in pieces])


def outer_kernel(x_ref, y_ref, *refs):
    outs, x_scr = refs[:-1], refs[-1]

    @pl.when(pl.program_id(0) == 0)
    def order():
        for p in range(x_ref.shape[1] // LANES):
            part = x_ref[:, place_of(p)].astype(jnp.float32)
            x_scr[pl.ds(p * LANES, LANES), :] = part.T.astype(x_scr.dtype)

    product = jnp.dot(x_scr[...], y_ref[...], preferred_element_type=jnp.float32)
    for p in range(product.shape[0] // LANES):
        row = (0, 2, 1, 3)[p // len(outs)] * LANES
        part = product[p * LANES : (p + 1) * LANES]
        outs[p % len(outs)][row : row + LANES, :] = part.astype(outs[0].dtype)


def outer(x, y, width=512):
    rows, features = x.shape
    channels = y.shape[1]
    stacked = features // 4
    return pl.pallas_call(
        outer_kernel,
        grid=(channels // width,),
        in_specs=[
            pl.BlockSpec((rows, features), lambda j: (0, 0)),
            pl.BlockSpec((rows, width), lambda j: (0, j)),
        ],
        out_specs=[pl.BlockSpec((stacked, width), lambda j: (0, j))] * 4,
        out_shape=[jax.ShapeDtypeStruct((stacked, channels), jnp.bfloat16)] * 4,
        scratch_shapes=[pltpu.VMEM((features, rows), x.dtype)],
        compiler_params=limits(48),
        name="outer",
    )(x, y)


def assemble_kernel(blocks, extra_ref, proj_ref, rest_ref, dt_ref):
    depth = dt_ref.shape[0] // (dt_ref.shape[1] // LANES)
    proj_blocks = proj_ref.shape[0] // NSTATE
    odd = lax.rem(lax.axis_index(DP), 2) == 1
    for p in range(0, 16, 2):
        slot = (p >> 2) + (p & 2) * 2
        for core in range(2):
            here = place_of(p + core)
            for b in range(blocks):
                block = extra_ref[core, slot, :NSTATE, cols(b)]
                row = (b if b < proj_blocks else b - proj_blocks) * NSTATE
                if b < proj_blocks:
                    proj_ref[row : row + NSTATE, here] = block
                else:
                    rest_ref[row : row + NSTATE, here] = block.astype(jnp.float32)
        own = extra_ref[0, slot, NSTATE:, :].astype(jnp.float32)[:depth]
        other = extra_ref[1, slot, NSTATE:, :].astype(jnp.float32)[:depth]
        pair = jnp.concatenate(
            [jnp.where(odd, other, own), jnp.where(odd, own, other)], axis=0
        ).astype(dt_ref.dtype)
        first = (lax.axis_index(DP) ^ p) // 2
        dt_ref[pl.ds(pl.multiple_of(first * 2 * depth, 2 * depth), 2 * depth), :] = pair


def assemble(extra, proj_rows, rest_rows):
    channels = extra.shape[-1]
    return pl.pallas_call(
        functools.partial(assemble_kernel, (proj_rows + rest_rows) // NSTATE),
        out_shape=[
            jax.ShapeDtypeStruct((proj_rows, channels), extra.dtype),
            f32(rest_rows, channels),
            jax.ShapeDtypeStruct((RANK, channels), extra.dtype),
        ],
        compiler_params=limits(40),
        name="assemble",
    )(extra)


def deal_kernel(proj_ref, dt_ref, rest_ref, out_ref):
    count = out_ref.shape[0]
    bits = count.bit_length() - 1
    depth = dt_ref.shape[0] // count
    proj_rows = proj_ref.shape[0]
    rest_row = proj_rows + dt_ref.shape[0]
    for n in range(count):
        piece = sum(1 << (bits - 1 - b) for b in range(bits) if n >> b & 1)
        out_ref[n, :proj_rows, :] = proj_ref[:, place_of(piece)].astype(out_ref.dtype)
        out_ref[n, rest_row:, :] = rest_ref[:, place_of(piece)].astype(out_ref.dtype)
        place = pl.ds(pl.multiple_of((lax.axis_index(DP) ^ piece) * depth, depth), depth)
        for k in range(0, count, 2):
            both = jnp.concatenate([dt_ref[place, cols(k)], dt_ref[place, cols(k + 1)]], axis=0)
            row = proj_rows + k * depth
            out_ref[n, row : row + 2 * depth, :] = both.astype(out_ref.dtype)


def deal(proj, dt, rest):
    rows = proj.shape[0] + dt.shape[0] + rest.shape[0]
    return pl.pallas_call(
        deal_kernel,
        out_shape=jax.ShapeDtypeStruct((proj.shape[1] // LANES, rows, LANES), jnp.bfloat16),
        compiler_params=limits(40),
        name="deal",
    )(proj, dt, rest)


EPSILON = 1e-05
RESET = 1e30


def shifted(block, axis, distance):
    devices = range(lax.axis_size(axis))
    route = [(i - distance, i) for i in devices if i - distance in devices]
    return lax.ppermute(block, axis, route)


def swapped(block, axis):
    return lax.ppermute(block, axis, [(0, 1), (1, 0)])


def exchanged(block, mask):
    return lax.ppermute(block, DP, [(i, i ^ mask) for i in range(lax.axis_size(DP))])


def after(block, *earlier):
    return lax.optimization_barrier((block, *earlier))[0] if earlier else block


def sent(block, mask, name, *earlier):
    with jax.named_scope(f"{name}_to_{mask}"):
        return exchanged(after(block, *earlier), mask)


def round_masks():
    return [1 << n for n in range(lax.axis_size(DP).bit_length() - 1)]


def total(*blocks):
    result = blocks[0].astype(jnp.float32)
    for block in blocks[1:]:
        result = result + block.astype(jnp.float32)
    return result


def silu_slope(values):
    squash = jax.nn.sigmoid(values)
    return squash * (1.0 + values * (1.0 - squash))


def dot(left, right, dims):
    return lax.dot_general(left, right, (dims, ((), ())), preferred_element_type=jnp.float32)


def joined(block, axis):
    if lax.axis_size(axis) != 2:
        return lax.all_gather(block, axis, axis=block.ndim - 1, tiled=True)
    other = swapped(block, axis)
    first = lax.axis_index(axis) == 0
    return jnp.concatenate(
        [jnp.where(first, block, other), jnp.where(first, other, block)], axis=-1
    )


def summed(block, axis):
    if lax.axis_size(axis) != 2:
        return lax.psum(block, axis)
    return block + swapped(block, axis)


def sum_scattered(block, axis):
    last = block.ndim - 1
    if lax.axis_size(axis) != 2:
        return lax.psum_scatter(block, axis, scatter_dimension=last, tiled=True)
    width = block.shape[-1] // 2
    place = lax.axis_index(axis)
    own = lax.dynamic_slice_in_dim(block, place * width, width, last)
    other = lax.dynamic_slice_in_dim(block, (1 - place) * width, width, last)
    return own + swapped(other, axis)


def entering(value, span, rate, axis, direction):
    value = shifted(value, axis, direction)
    span = shifted(span, axis, direction)
    distance = 1
    while distance < lax.axis_size(axis):
        further = shifted(value, axis, direction * distance)
        further_span = shifted(span, axis, direction * distance)
        value = value + jnp.exp2(rate[None] * span[:, None, :]) * further
        span = span + further_span
        distance *= 2
    return value


def local_whole(
    tokens, segments, cotangent, norm_gain, w_in, conv_w, conv_b, w_x, w_dt, dt_bias, a_log, d_skip, w_out
):
    seqs, rows, part = tokens.shape
    features, channels = part * lax.axis_size(TENSOR), w_in.shape[2]
    devices = lax.axis_size(DP)
    shard = channels // devices
    taps = conv_w.shape[0]
    reach = taps - 1
    block = min(512, channels)
    count = seqs * rows
    low = jnp.bfloat16

    small = jnp.concatenate(
        [
            conv_w,
            conv_b[None],
            dt_bias[None],
            d_skip[None],
            a_log.T,
            w_x.T,
            w_dt.reshape(-1, shard),
            norm_gain.reshape(-1, shard),
        ],
        axis=0,
    )
    small = lax.all_gather(small, DP)
    w_in_x = lax.all_gather(w_in[:, 0], DP, axis=0, tiled=True)
    w_in_gate = lax.all_gather(w_in[:, 1], DP, axis=0, tiled=True)
    w_out_t = lax.all_gather(w_out.T, DP, axis=0, tiled=True)
    channel_rows = taps + 3 + NSTATE + w_x.shape[1]
    by_channel = small[:, :channel_rows].transpose(1, 0, 2).reshape(channel_rows, channels)
    taps_f = by_channel[:taps].astype(jnp.float32)
    bias_f, shift_f, skip_f = (by_channel[taps + i].astype(jnp.float32)[None] for i in range(3))
    a_mat = -jnp.exp(by_channel[taps + 3 : taps + 3 + NSTATE].astype(jnp.float32))
    rate = a_mat * LOG2E
    w_x_t = by_channel[taps + 3 + NSTATE :]
    dt_full = small[:, channel_rows : channel_rows + RANK].reshape(RANK, channels)
    gain_f = small[:, channel_rows + RANK :].reshape(features).astype(jnp.float32)

    marks_own = segments + 1
    marks_before = shifted(marks_own[:, rows - reach :], DP, 1)
    marks = jnp.concatenate([marks_before, marks_own], axis=1)
    tail = shifted(tokens[:, rows - reach :], DP, 1)
    wanted = jnp.concatenate(
        [tokens.reshape(count, part), tail.reshape(seqs * reach, part)], axis=0
    )
    x_rows = joined(wanted, TENSOR).astype(jnp.float32)
    cot = joined(cotangent.reshape(count, part), TENSOR)
    scale_all = lax.rsqrt(jnp.mean(x_rows * x_rows, axis=1, keepdims=True) + EPSILON)
    normed_all = (x_rows * scale_all * gain_f[None]).astype(low)
    normed, scale = normed_all[:count], scale_all[:count]

    inner_all = dot(normed_all, w_in_x, ((1,), (0,))).astype(low)
    inner_ext = jnp.concatenate(
        [
            inner_all[count:].reshape(seqs, reach, channels),
            inner_all[:count].reshape(seqs, rows, channels),
        ],
        axis=1,
    ).astype(jnp.float32)
    tap_masks = [
        (marks[:, k : k + rows] == marks_own).astype(jnp.float32)[:, :, None] for k in range(taps)
    ]
    mixed = bias_f[None]
    for k in range(taps):
        mixed = mixed + taps_f[k][None, None] * inner_ext[:, k : k + rows] * tap_masks[k]
    conv_low = jax.nn.silu(mixed).astype(low)
    conv = conv_low.astype(jnp.float32)
    conv_flat = conv_low.reshape(count, channels)
    proj = summed(dot(conv_flat, w_x_t, ((1,), (1,))), TENSOR)
    rank_part = proj[:, :RANK].astype(low)
    bc = jnp.broadcast_to(
        proj[:, RANK:].reshape(seqs, rows, 2 * NSTATE, 1), (seqs, rows, 2 * NSTATE, LANES)
    )
    pre = (dot(rank_part, dt_full, ((1,), (0,))) + shift_f).reshape(seqs, rows, channels)
    delta = jax.nn.softplus(pre)
    step = jnp.where(tap_masks[reach - 1] > 0, delta, RESET)
    flow = delta * conv
    span = jnp.sum(step, axis=1)

    end = forward_end(step, flow, bc, rate, block)
    enter = entering(end, span, rate, DP, 1)
    readout = forward_main(step, flow, bc, rate, enter, block)
    ssm = readout + skip_f[None] * conv

    gate = dot(normed, w_in_gate, ((1,), (0,))).reshape(seqs, rows, channels)
    silu_gate = jax.nn.silu(gate)
    gated = (ssm * silu_gate).astype(low).reshape(count, channels)
    branch = sum_scattered(dot(gated, w_out_t, ((1,), (1,))), TENSOR)
    tokens_f = tokens.reshape(count, part).astype(jnp.float32)
    block_out = (tokens_f + branch).astype(low).reshape(seqs, rows, part)
    grad_out_t = dot(cot, gated, ((0,), (0,))).astype(low)
    grad_out_t = lax.psum_scatter(grad_out_t, DP, scatter_dimension=0, tiled=True)
    grad_gated = dot(cot, w_out_t, ((1,), (0,))).reshape(seqs, rows, channels)
    grad_ssm = grad_gated * silu_gate
    grad_gate = (grad_gated * ssm * silu_slope(gate)).astype(low).reshape(count, channels)
    grad_in_gate = dot(normed, grad_gate, ((0,), (0,))).astype(low)
    grad_in_gate = lax.psum_scatter(grad_in_gate, DP, scatter_dimension=0, tiled=True)
    grad_skip = jnp.sum(grad_ssm * conv, axis=(0, 1))

    back_end = reverse_end(step, grad_ssm, bc, rate, block)
    leave = entering(back_end, span, rate, DP, -1)
    back = ()
    for n in range(seqs):
        back = reverse_main(
            step, delta, flow, conv, grad_ssm, bc, rate, a_mat, enter, leave, block, n, back
        )
    grad_delta, grad_conv_scan, grad_bc, grad_a = back
    grad_delta, grad_conv_scan = (part.reshape(step.shape) for part in (grad_delta, grad_conv_scan))
    grad_alog = jnp.sum(grad_a, axis=0) * a_mat
    grad_pre = grad_delta * jax.nn.sigmoid(pre)
    grad_shift = jnp.sum(grad_pre, axis=(0, 1))
    grad_pre_low = grad_pre.astype(low).reshape(count, channels)
    grad_dt = dot(rank_part, grad_pre_low, ((0,), (0,)))
    grad_rank = dot(grad_pre_low, dt_full, ((1,), (1,)))
    grad_proj = jnp.concatenate(
        [grad_rank, jnp.sum(grad_bc, axis=-1).reshape(count, 2 * NSTATE)], axis=1
    )
    grad_proj = summed(grad_proj, TENSOR).astype(low)
    grad_x_t = dot(grad_proj, conv_flat, ((0,), (0,)))
    grad_conv = (
        grad_conv_scan
        + skip_f[None] * grad_ssm
        + dot(grad_proj, w_x_t, ((1,), (0,))).reshape(seqs, rows, channels)
    )
    grad_mixed = grad_conv * silu_slope(mixed)
    grad_bias = jnp.sum(grad_mixed, axis=(0, 1))
    grad_taps = jnp.stack(
        [
            jnp.sum(grad_mixed * inner_ext[:, k : k + rows] * tap_masks[k], axis=(0, 1))
            for k in range(taps)
        ]
    )
    grad_ext = jnp.zeros((seqs, rows + reach, channels), jnp.float32)
    for k in range(taps):
        grad_ext = grad_ext + jnp.pad(
            taps_f[k][None, None] * grad_mixed * tap_masks[k], ((0, 0), (k, reach - k), (0, 0))
        )
    returned = shifted(grad_ext[:, :reach], DP, -1)
    grad_inner = grad_ext[:, reach:] + jnp.pad(returned, ((0, 0), (rows - reach, 0), (0, 0)))
    grad_inner = grad_inner.astype(low).reshape(count, channels)
    grad_in_x = dot(normed, grad_inner, ((0,), (0,))).astype(low)
    grad_in_x = lax.psum_scatter(grad_in_x, DP, scatter_dimension=0, tiled=True)

    grad_normed = sum_scattered(
        dot(grad_inner, w_in_x, ((1,), (1,))) + dot(grad_gate, w_in_gate, ((1,), (1,))), TENSOR
    )
    column = lax.axis_index(TENSOR) * part
    gain_local = lax.dynamic_slice_in_dim(gain_f, column, part, 0)
    weighted = grad_normed * gain_local[None]
    grad_gain = jnp.sum(grad_normed * tokens_f * scale, axis=0)
    grad_gain = lax.dynamic_update_slice_in_dim(
        jnp.zeros((features,), jnp.float32), grad_gain, column, 0
    )
    row_total = summed(jnp.sum(weighted * tokens_f, axis=1, keepdims=True), TENSOR)
    input_grad = (
        cotangent.reshape(count, part).astype(jnp.float32)
        + scale * weighted
        - tokens_f * (scale * scale * scale) * (row_total / features)
    ).reshape(seqs, rows, part)

    by_channel = jnp.concatenate(
        [grad_taps, grad_bias[None], grad_shift[None], grad_skip[None], grad_alog, grad_x_t], axis=0
    )
    by_channel = by_channel.reshape(channel_rows, devices, shard).transpose(1, 0, 2)
    packed = jnp.concatenate(
        [
            by_channel,
            grad_dt.reshape(devices, RANK, shard),
            grad_gain.reshape(devices, -1, shard),
        ],
        axis=1,
    )
    packed = lax.psum_scatter(packed, DP, scatter_dimension=0)
    by_channel = packed[:channel_rows]
    grad_dt = packed[channel_rows : channel_rows + RANK].reshape(-1, channels)
    grad_gain = summed(packed[channel_rows + RANK :], TENSOR).reshape(-1)
    grad_in = jnp.stack([grad_in_x, grad_in_gate], axis=1).astype(jnp.float32)
    return (
        block_out,
        input_grad,
        grad_gain,
        grad_in,
        by_channel[:taps],
        by_channel[taps],
        by_channel[taps + 3 + NSTATE :].T,
        grad_dt,
        by_channel[taps + 1],
        by_channel[taps + 3 : taps + 3 + NSTATE].T,
        by_channel[taps + 2],
        grad_out_t.astype(jnp.float32).T,
    )


class Names:
    def __getattr__(self, name):
        return name


N = Names()


class Plan:
    def __init__(self, waits):
        self.waits, self.steps, self.values, self.open = waits, {}, {}, set()

    def add(self, name, step):
        self.steps[name] = step

    def get(self, name):
        if name not in self.values:
            if name in self.open:
                raise ValueError(f"cycle at {name}")
            self.open.add(name)
            self.values[name] = self.steps[name]()
            self.open.remove(name)
        return self.values[name]

    def first(self, name):
        value = self.get(name)
        return value[0] if isinstance(value, (tuple, list)) else value

    def tied(self, name, block):
        return after(block, *(self.first(other) for other in self.waits.get(name, ())))

    def send(self, name, block, mask):
        def step():
            with jax.named_scope(name):
                return exchanged(self.tied(name, block()), mask)

        self.add(name, step)

    def swap(self, name, block):
        def step():
            with jax.named_scope(name):
                return swapped(self.tied(name, block()), TENSOR)

        self.add(name, step)


def gather_steps(plan, chunk, shard, groups, rows):
    places = {}

    def block(pieces):
        parts = []
        for n, piece in enumerate(pieces):
            name, row = places[piece]
            array = plan.get(name) if name else shard()
            part = array[row * LANES : row * LANES + rows] if array.shape[0] != rows else array
            parts.append(part)
        return parts[0] if len(parts) == 1 else jnp.concatenate(parts, axis=0)

    def move(name, pieces, mask):
        def start():
            return block(pieces)

        plan.send(name, start, mask)
        for n, piece in enumerate(pieces):
            places[piece + mask] = (name, n)

    places[0] = (None, 0)
    move(f"{chunk}4", (0,), 4)
    move(f"{chunk}8", (0,), 8)
    move(f"{chunk}12", (8,), 4)
    for group in groups:
        move(f"{chunk}x{group[0]}", group, 2)

    def core(name, pieces):
        first, *others = (block((p,))[:LANES] for p in pieces)
        return jnp.concatenate([plan.tied(name, first), *others], axis=0)

    for x in (0, 2):
        name, pieces = f"{chunk}s{x}", [z + x for z in (0, 4, 8, 12)]
        plan.send(name, lambda name=name, pieces=pieces: core(name, pieces), 1)
        for n, piece in enumerate(pieces):
            places[piece + 1] = (name, n)

    def pieces():
        return [(plan.get(places[p][0]) if places[p][0] else shard(), places[p][1]) for p in range(16)]

    def extra():
        return jnp.stack([block((p,))[LANES:] for p in (0, 4, 8, 12, 2, 6, 10, 14)])

    plan.add(chunk, pieces)
    if rows > LANES:
        plan.add(f"{chunk}own", extra)
        plan.send(f"{chunk}e", lambda: plan.get(f"{chunk}own"), 1)


ROWS = {0: 0, 8: 1, 4: 2, 12: 3}


def scatter_steps(plan, name, outer_name, groups, near_groups):
    crossed, neared = {}, {}

    def rows_of(group):
        first = ROWS[group[0]]
        return slice(first * LANES, (first + len(group)) * LANES)

    def chip(x, group):
        return [plan.get(outer_name)[x][rows_of(group)], plan.get(f"{name}s{x}")[rows_of(group)]]

    def pick(table, z):
        step, n = table[z]
        return plan.get(step)[n * LANES : (n + 1) * LANES]

    for x in (2, 0):
        plan.send(f"{name}s{x}", lambda x=x: plan.get(outer_name)[x + 1], 1)
    for group in groups:
        ready, step = f"{name}p{group[0]}", f"{name}x{group[0]}"
        plan.add(ready, lambda group=group: total(*chip(2, group)).astype(jnp.bfloat16))
        plan.send(step, lambda ready=ready: plan.get(ready), 2)
        for n, z in enumerate(group):
            crossed[z] = (step, n)

    def column(group):
        parts = [
            total(*chip(0, (z,)), pick(crossed, z), *([pick(neared, z)] if z == 8 else [])) for z in group
        ]
        return jnp.concatenate(parts, axis=0).astype(jnp.bfloat16)

    for group in near_groups:
        step = f"{name}z{group[0]}"
        plan.send(step, lambda group=group: column(group), 4)
        for n, z in enumerate(group):
            neared[z - 4] = (step, n)
    plan.send(f"{name}z8", lambda: column((8,)), 8)

    def result():
        last = plan.tied(name, plan.get(f"{name}z8"))
        return total(last, pick(neared, 0), pick(crossed, 0), *chip(0, (0,)))

    plan.add(name, result)


def state_steps(plan, name, value, span, rate, known=None):
    low = jnp.bfloat16

    def message(n):
        mask = round_masks()[n]
        lower = lax.rem(lax.div(lax.axis_index(DP), mask), 2) == 0
        now = plan.get(f"{name}in{n}")
        got = plan.get(f"{name}{n}")
        other = got[:, :NSTATE].astype(jnp.float32)
        own_span, other_span, before, behind = plan.get(f"{known or name}spans{n}")
        first = ~lower if known else lower
        far = jnp.where(first, 0.0, other)
        decay = lambda steps: jnp.exp2(rate()[None] * steps[:, None, :])
        result = far if n == 0 else now[1] + decay(behind if known else before) * far
        through = jnp.where(first, other_span, own_span)
        value = jnp.where(first, other, now[0]) + decay(through) * jnp.where(first, now[0], other)
        return value, result

    def spans(n):
        if n == 0:
            own, before, behind = span(), jnp.zeros_like(span()), jnp.zeros_like(span())
        else:
            own, other, before, behind = plan.get(f"{name}spans{n - 1}")
            lower = lax.rem(lax.div(lax.axis_index(DP), round_masks()[n - 1]), 2) == 0
            before = before + jnp.where(lower, 0.0, other)
            behind = behind + jnp.where(lower, other, 0.0)
            own = own + other
        with jax.named_scope(f"{name}span{n}"):
            other = exchanged(plan.tied(f"{name}span{n}", own), round_masks()[n])
        return own, other, before, behind

    count = len(round_masks())
    for n in range(count):
        plan.add(f"{name}in{n}", lambda n=n: message(n - 1) if n else (value(), None))
        plan.send(f"{name}{n}", lambda n=n: plan.get(f"{name}in{n}")[0].astype(low), round_masks()[n])
        if not known:
            plan.add(f"{name}spans{n}", lambda n=n: spans(n))
    plan.add(name, lambda: message(count - 1)[1])


def pack_steps(plan, name, blocks):
    def sums(n):
        if n == 0:
            return blocks()
        before = sums_of(n - 1)
        half = before.shape[0] // 2
        return before[:half].astype(jnp.float32) + plan.get(f"{name}{n - 1}").astype(jnp.float32)

    def sums_of(n):
        return plan.get(f"{name}sum{n}")

    def sent_half(n):
        block = sums_of(n)
        return block[block.shape[0] // 2 :].astype(jnp.bfloat16)

    for n in range(len(round_masks()) + 1):
        plan.add(f"{name}sum{n}", lambda n=n: sums(n))
    for n, mask in enumerate(round_masks()):
        plan.send(f"{name}{n}", lambda n=n: sent_half(n), mask)
    plan.add(name, lambda: sums_of(len(round_masks()))[0])


WAITS = dict(
    a12=(N.a4, N.a8, N.ax0, N.bx0),
    ax4=(N.a4, N.a8, N.ax0, N.bx0),
    ax8=(N.a4, N.a8, N.ax0, N.bx0),
    b4=(N.a12,),
    b8=(N.a12,),
    ax12=(N.ax4, N.ax8, N.a12),
    as0=(N.ax4, N.ax8, N.a12),
    as2=(N.b4, N.b8),
    bx4=(N.as0, N.as2, N.ae),
    bx8=(N.inner, N.ax12),
    b12=(N.inner, N.ax12),
    bx12=(N.inner, N.bx4),
    bs0=(N.inner,),
    end=(N.bx8,),
    f1=(N.bx12,),
    gate=(N.f0,),
    readout=(N.gate,),
    outB=(N.r0,),
    branch=(N.outB,),
    back0=(N.branch,),
    taps=(N.grad_normed,),
    c=(N.inner,),
    grad_gated=(N.outC,),
    back1=(N.Bx4,),
    grad_pre=(N.Bx0,),
    grad_mixed=(N.Bz4,),
    Bz8=(N.Ap4,),
    down=(N.Ap4,),
    Ax0=(N.Ap4,),
    yn=(N.Ax4, N.Bz8),
    y0=(N.ax0,),
)
GROUPS = dict(
    a=((0,), (4,), (8,), (12,)),
    b=((0,), (4,), (8,), (12,)),
    c=(),
    C=(),
    B=((4, 12), (0, 8)),
    A=((4, 12), (0, 8)),
    Cz=(),
    Bz=((4, 12),),
    Az=((12,), (4,)),
)


def local(
    tokens, segments, cotangent, norm_gain, w_in, conv_w, conv_b, w_x, w_dt, dt_bias, a_log, d_skip, w_out
):
    seqs, rows, part = tokens.shape
    features, channels = part * 2, w_in.shape[2]
    devices = lax.axis_size(DP)
    shard = channels // devices
    taps = conv_w.shape[0]
    reach = taps - 1
    block = min(512, channels)
    count = seqs * rows
    low = jnp.bfloat16
    plan = Plan(WAITS)
    get, add, tied = plan.get, plan.add, plan.tied
    first_half = lax.axis_index(TENSOR) == 0

    def natural(own, other):
        return jnp.concatenate(
            [jnp.where(first_half, own, other), jnp.where(first_half, other, own)], axis=-1
        )

    def up_any(x, weights):
        if isinstance(weights, list):
            return up(x, weights, jnp.float32)
        return dot(x, weights, ((1,), (0,)))

    def pieces_of(weights):
        return weights if isinstance(weights, list) else [(weights, None)] * devices

    proj_rows = w_x.shape[1]
    small = jnp.concatenate(
        [
            w_x.T,
            a_log.T,
            conv_w,
            conv_b[None],
            dt_bias[None],
            d_skip[None],
            norm_gain.reshape(-1, shard),
        ],
        axis=0,
    )
    rest_rows = small.shape[0] - proj_rows
    rest_rows += -rest_rows % NSTATE
    small = jnp.pad(small, ((0, channels // LANES * NSTATE - small.shape[0]), (0, 0)))
    small = small.reshape(-1, NSTATE, LANES).transpose(1, 0, 2).reshape(NSTATE, channels)
    steps = jnp.pad(w_dt, ((0, NSTATE - w_dt.shape[0]), (0, 0)))
    shard_x = jnp.concatenate([w_in[:, 0], small, steps], axis=0)
    shard_gate, shard_out = w_in[:, 1], w_out.T
    gather_steps(plan, N.a, lambda: shard_x, GROUPS[N.a], shard_x.shape[0])
    for name, held in ((N.b, shard_gate), (N.c, shard_out)):
        if GROUPS[name]:
            gather_steps(plan, name, lambda held=held: held, GROUPS[name], LANES)
        else:
            add(name, lambda name=name, held=held: lax.all_gather(tied(name, held), DP, axis=0, tiled=True))

    def small_weights():
        extra = jnp.stack([get(N.aown), get(N.ae)])
        w_x_t, rest, dt_full = assemble(tied(N.small, extra), proj_rows, rest_rows)
        a_mat = -jnp.exp(rest[:NSTATE])
        gain = rest[NSTATE + taps + 3]
        others = [rest[NSTATE + taps + i][None] for i in range(3)]
        return w_x_t, dt_full, a_mat, a_mat * LOG2E, rest[NSTATE : NSTATE + taps], gain, *others

    add(N.small, small_weights)

    marks_own = segments + 1
    marks_before = shifted(marks_own[:, rows - reach :], DP, 1)
    marks = jnp.concatenate([marks_before, marks_own], axis=1)
    tap_masks = [
        (marks[:, k : k + rows] == marks_own).astype(jnp.float32)[:, :, None] for k in range(taps)
    ]
    tail = shifted(tokens[:, rows - reach :], DP, 1)
    wanted = [cotangent.reshape(count, part), tokens.reshape(count, part)]
    wanted.append(tail.reshape(seqs * reach, part))
    wanted = jnp.concatenate(wanted, axis=0)
    wanted = jnp.pad(wanted, ((0, -wanted.shape[0] % 16), (0, 0)))
    tokens_f = tokens.reshape(count, part).astype(jnp.float32)
    plan.swap(N.y0, lambda: wanted)
    add(N.rows, lambda: natural(wanted, get(N.y0)))

    def normed():
        x_rows = get(N.rows)[count:].astype(jnp.float32)
        scale = lax.rsqrt(jnp.mean(x_rows * x_rows, axis=1, keepdims=True) + EPSILON)
        return (x_rows * scale * get(N.small)[5][None]).astype(low), scale

    add(N.normed, normed)
    add(N.cot, lambda: get(N.rows)[:count])

    add(N.inner, lambda: up(tied(N.inner, get(N.normed)[0]), get(N.a), low))

    def extended():
        inner = get(N.inner)
        before = inner[count : count + seqs * reach].reshape(seqs, reach, channels)
        now = inner[:count].reshape(seqs, rows, channels)
        return jnp.concatenate([before, now], axis=1).astype(jnp.float32)

    add(N.extended, extended)

    def mixed():
        taps_f, bias_f = get(N.small)[4], get(N.small)[6]
        result = bias_f[None]
        for k in range(taps):
            result = result + taps_f[k][None, None] * get(N.extended)[:, k : k + rows] * tap_masks[k]
        return result

    add(N.mixed, mixed)
    add(N.conv, lambda: jax.nn.silu(get(N.mixed)).astype(low))
    add(N.conv_flat, lambda: get(N.conv).reshape(count, channels))
    add(N.part, lambda: dot(get(N.conv_flat), get(N.small)[0], ((1,), (1,))))
    plan.swap(N.yp, lambda: get(N.part))
    add(N.proj, lambda: get(N.part) + get(N.yp))
    add(N.rank, lambda: get(N.proj)[:, :RANK].astype(low))

    def broadcast():
        columns = get(N.proj)[:, RANK:].reshape(seqs, rows, 2 * NSTATE, 1)
        return jnp.broadcast_to(columns, (seqs, rows, 2 * NSTATE, LANES))

    add(N.bc, broadcast)

    def pre():
        product = dot(get(N.rank), get(N.small)[1], ((1,), (0,)))
        return (product + get(N.small)[7]).reshape(seqs, rows, channels)

    add(N.pre, pre)
    add(N.delta, lambda: jax.nn.softplus(get(N.pre)))
    add(N.step, lambda: jnp.where(tap_masks[reach - 1] > 0, get(N.delta), RESET))
    add(N.flow, lambda: get(N.delta) * get(N.conv).astype(jnp.float32))
    add(N.span, lambda: jnp.sum(get(N.step), axis=1))

    def rate():
        return get(N.small)[3]

    add(N.end, lambda: forward_end(get(N.step), tied(N.end, get(N.flow)), get(N.bc), rate(), block))
    state_steps(plan, N.f, lambda: get(N.end), lambda: get(N.span), rate)
    add(N.enter, lambda: get(N.f))
    add(
        N.readout,
        lambda: forward_main(
            get(N.step), get(N.flow), get(N.bc), rate(), tied(N.readout, get(N.enter)), block
        ),
    )
    add(N.ssm, lambda: get(N.readout) + get(N.small)[8][None] * get(N.conv).astype(jnp.float32))

    def gate():
        own = tied(N.gate, get(N.normed)[0][:count])
        return up_any(own, get(N.b)).reshape(seqs, rows, channels)

    add(N.gate, gate)
    add(N.silu_gate, lambda: jax.nn.silu(get(N.gate)))
    add(N.gated, lambda: (get(N.ssm) * get(N.silu_gate)).astype(low).reshape(count, channels))
    def scatter(name, x, y, groups, near):
        if groups:
            add(f"out{name}", lambda: outer(x(), y()))
            scatter_steps(plan, name, f"out{name}", groups, near)
        else:
            add(f"out{name}", lambda: dot(x(), y(), ((0,), (0,))).astype(low))
            add(f"{name}rs", lambda: lax.psum_scatter(get(f"out{name}"), DP, scatter_dimension=0, tiled=True))
            add(name, lambda: tied(name, get(f"{name}rs")).astype(jnp.float32))

    scatter(N.C, lambda: get(N.cot), lambda: tied(N.outC, get(N.gated)), GROUPS[N.C], GROUPS[N.Cz])
    add(N.grad_gated, lambda: up_any(tied(N.grad_gated, get(N.cot)), get(N.c)))
    add(N.grad_gated3, lambda: get(N.grad_gated).reshape(seqs, rows, channels))
    add(N.grad_ssm, lambda: tied(N.grad_ssm, get(N.grad_gated3)) * get(N.silu_gate))

    def grad_gate():
        slope = silu_slope(get(N.gate))
        result = tied(N.grad_gate, get(N.grad_gated3)) * get(N.ssm) * slope
        return result.astype(low).reshape(count, channels)

    add(N.grad_gate, grad_gate)

    add(
        N.rend,
        lambda: reverse_end(get(N.step), tied(N.rend, get(N.grad_ssm)), get(N.bc), rate(), block),
    )
    state_steps(plan, N.r, lambda: get(N.rend), None, rate, N.f)
    scatter(N.B, lambda: get(N.normed)[0][:count], lambda: tied(N.outB, get(N.grad_gate)), GROUPS[N.B], GROUPS[N.Bz])
    add(N.branch, lambda: down([(tied(N.branch, get(N.gated)), pieces_of(get(N.c)))], low))
    plan.swap(N.yb, lambda: get(N.branch)[1])

    def back(n):
        into = get(f"back{n - 1}") if n else ()
        leave = tied(f"back{n}", get(N.r))
        inputs = [get(N.step), get(N.delta), get(N.flow)]
        inputs += [get(N.conv).astype(jnp.float32), get(N.grad_ssm), get(N.bc), rate()]
        inputs += [get(N.small)[2], get(N.enter), leave]
        return reverse_main(*inputs, block, n, into)

    for n in range(seqs):
        add(f"back{n}", lambda n=n: back(n))

    def back_all(n):
        result = get(f"back{seqs - 1}")[n]
        return result.reshape(seqs, rows, channels) if n < 2 else result

    add(N.grad_pre, lambda: tied(N.grad_pre, back_all(0)) * jax.nn.sigmoid(get(N.pre)))
    add(N.grad_pre_low, lambda: get(N.grad_pre).astype(low).reshape(count, channels))

    def proj_part():
        grad_rank = dot(get(N.grad_pre_low), get(N.small)[1], ((1,), (1,)))
        grad_bc = jnp.sum(back_all(2), axis=-1).reshape(count, 2 * NSTATE)
        return jnp.concatenate([grad_rank, grad_bc], axis=1)

    add(N.gpart, proj_part)
    plan.swap(N.yg, lambda: get(N.gpart))
    add(N.grad_proj, lambda: (get(N.gpart) + get(N.yg)).astype(low))

    def grad_mixed():
        product = dot(tied(N.grad_mixed, get(N.grad_proj)), get(N.small)[0], ((1,), (0,)))
        grad_conv = back_all(1) + get(N.small)[8][None] * get(N.grad_ssm)
        grad_conv = grad_conv + product.reshape(seqs, rows, channels)
        return grad_conv * silu_slope(get(N.mixed))

    add(N.grad_mixed, grad_mixed)

    def grad_ext():
        grads = tied(N.grad_ext, get(N.grad_mixed))
        result = jnp.zeros((seqs, rows + reach, channels), jnp.float32)
        for k in range(taps):
            term = get(N.small)[4][k][None, None] * grads * tap_masks[k]
            result = result + jnp.pad(term, ((0, 0), (k, reach - k), (0, 0)))
        return result

    add(N.grad_ext, grad_ext)
    add(N.returned, lambda: shifted(get(N.grad_ext)[:, :reach], DP, -1))

    def grad_inner():
        returned = jnp.pad(get(N.returned), ((0, 0), (rows - reach, 0), (0, 0)))
        result = get(N.grad_ext)[:, reach:] + returned
        return result.astype(low).reshape(count, channels)

    add(N.grad_inner, grad_inner)
    scatter(N.A, lambda: get(N.normed)[0][:count], lambda: tied(N.outA, get(N.grad_inner)), GROUPS[N.A], GROUPS[N.Az])

    def grad_rows():
        pairs = [(tied(N.down, get(N.grad_inner)), get(N.a)), (get(N.grad_gate), pieces_of(get(N.b)))]
        return down(pairs, low)

    add(N.down, grad_rows)
    plan.swap(N.yn, lambda: get(N.down)[1])
    add(N.grad_normed, lambda: tied(N.grad_normed, get(N.down)[0] + get(N.yn).astype(jnp.float32)))
    column = lax.axis_index(TENSOR) * part
    scale = get(N.normed)[1][:count]
    add(N.weighted, lambda: get(N.grad_normed) * lax.dynamic_slice_in_dim(get(N.small)[5], column, part, 0)[None])
    add(N.row_part, lambda: jnp.sum(get(N.weighted) * tokens_f, axis=1, keepdims=True))
    plan.swap(N.yt, lambda: get(N.row_part))

    def input_grad():
        row_total = get(N.row_part) + get(N.yt)
        grads = scale * get(N.weighted) - tokens_f * (scale * scale * scale) * (row_total / features)
        return (cotangent.reshape(count, part).astype(jnp.float32) + grads).reshape(seqs, rows, part)

    def block_out():
        branch = tied(N.block_out, get(N.branch)[0]) + get(N.yb).astype(jnp.float32)
        return (tokens_f + branch).astype(low).reshape(seqs, rows, part)

    def small_grads():
        own, other = get(N.down)
        grads = natural(own, other.astype(jnp.float32))
        x_rows = get(N.rows)[count : 2 * count].astype(jnp.float32)
        grad_gain = jnp.sum(grads * x_rows * scale, axis=0)
        grads = tied(N.taps, get(N.grad_mixed))
        rest = [
            jnp.sum(grads * get(N.extended)[:, k : k + rows] * tap_masks[k], axis=(0, 1))
            for k in range(taps)
        ]
        rest.append(jnp.sum(grads, axis=(0, 1)))
        rest.append(jnp.sum(tied(N.shift, get(N.grad_pre)), axis=(0, 1)))
        conv = get(N.conv).astype(jnp.float32)
        rest.append(jnp.sum(tied(N.skip, get(N.grad_ssm)) * conv, axis=(0, 1)))
        rest.append(grad_gain)
        grad_alog = jnp.sum(back_all(3), axis=0) * get(N.small)[2]
        rest = jnp.concatenate([grad_alog, jnp.stack(rest)], axis=0)
        rest = jnp.pad(rest, ((0, -rest.shape[0] % 16), (0, 0)))
        grad_x_t = dot(tied(N.grad_x, get(N.grad_proj)), get(N.conv_flat), ((0,), (0,)))
        grad_dt = dot(tied(N.grad_dt, get(N.rank)), get(N.grad_pre_low), ((0,), (0,)))
        return deal(grad_x_t, grad_dt, rest)

    pack_steps(plan, N.k, small_grads)
    input_grad, block_out = input_grad(), block_out()
    packed = get(N.k)
    grad_dt = packed[proj_rows : proj_rows + RANK].reshape(devices, -1, shard)
    grad_dt = grad_dt.transpose(1, 0, 2).reshape(-1, channels)
    rest = packed[proj_rows + RANK :]
    by_channel = rest[NSTATE:]
    gain_part = by_channel[taps + 3]
    grad_gain = gain_part + swapped(gain_part, TENSOR)
    grad_in = jnp.stack([get(N.A), get(N.B)], axis=1)
    return (
        block_out,
        input_grad,
        grad_gain,
        grad_in,
        by_channel[:taps],
        by_channel[taps],
        packed[:proj_rows].T,
        grad_dt,
        by_channel[taps + 1],
        rest[:NSTATE].T,
        by_channel[taps + 2],
        get(N.C).T,
    )


def solution(mesh):
    both = (TENSOR, DP)
    devices, halves = mesh.shape[DP], mesh.shape[TENSOR]

    def run(tokens, segments, cotangent, norm_gain, w_in, *others):
        trees = devices == 16 and halves == 2 and w_in.shape[0] == devices * LANES
        trees = trees and w_in.shape[2] == halves * devices * LANES
        return sharded(local if trees else local_whole)(
            tokens, segments, cotangent, norm_gain, w_in, *others
        )

    def sharded(function):
        return jax.shard_map(
            function,
            mesh=mesh,
            in_specs=(
                P(None, DP, TENSOR),
                P(None, DP),
                P(None, DP, TENSOR),
                P(DP),
                P(DP, None, TENSOR),
                P(None, both),
                P(both),
                P(both, None),
                P(DP, TENSOR),
                P(both),
                P(both, None),
                P(both),
                P(TENSOR, DP),
            ),
            out_specs=(
                P(None, DP, TENSOR),
                P(None, DP, TENSOR),
                P(DP),
                P(DP, None, TENSOR),
                P(None, both),
                P(both),
                P(both, None),
                P(DP, TENSOR),
                P(both),
                P(both, None),
                P(both),
                P(TENSOR, DP),
            ),
            check_vma=False,
        )

    return run
```

```python
import functools

import jax
import jax.numpy as jnp
from jax import lax
from jax.experimental import pallas as pl
from jax.experimental.pallas import tpu as pltpu
from jax.sharding import PartitionSpec as P

NSTATE = 16
RANK = 128
LANES = 128
DP = "dp"
TENSOR = "tensor"
GROUP = 8
LOG2E = 1.4426950408889634


def fold(parts, masks):
    width = 1
    while len(parts) > 1:
        joined = []
        for first, second in zip(parts[0::2], parts[1::2]):
            mask = masks[width]
            joined.append(
                jnp.where(mask, first, second) + pltpu.roll(jnp.where(mask, second, first), width, 0)
            )
        parts = joined
        width *= 2
    return parts[0]


def fold_masks():
    row = lax.broadcasted_iota(jnp.int32, (GROUP, LANES), 0)
    return {width: (row & width) == 0 for width in (1, 2, 4)}


def halves(value):
    return value[:GROUP] + value[GROUP:]


def spread(row):
    return jnp.broadcast_to(row, (NSTATE, LANES))


def cols(k):
    return pl.ds(k * LANES, LANES)


def forward_end_kernel(step_ref, flow_ref, b_ref, rate_ref, end_ref):
    groups, unused, width = step_ref.shape
    tiles = width // LANES
    rates = [rate_ref[:, cols(k)] for k in range(tiles)]

    def body(group, states):
        states = list(states)
        for j in range(GROUP):
            t = group * GROUP + j
            b_now = b_ref[t, :NSTATE, :]
            for k in range(tiles):
                decay = jnp.exp2(rates[k] * spread(step_ref[group, j : j + 1, cols(k)]))
                states[k] = decay * states[k] + b_now * spread(flow_ref[group, j : j + 1, cols(k)])
        return tuple(states)

    start = tuple(jnp.zeros((NSTATE, LANES), jnp.float32) for _ in range(tiles))
    ends = lax.fori_loop(0, groups, body, start)
    for k in range(tiles):
        end_ref[:, cols(k)] = ends[k]


def reverse_end_kernel(step_ref, grad_ref, c_ref, rate_ref, end_ref):
    groups, unused, width = step_ref.shape
    tiles = width // LANES
    rates = [rate_ref[:, cols(k)] for k in range(tiles)]

    def body(lap, states):
        states = list(states)
        group = groups - 1 - lap
        for j in reversed(range(GROUP)):
            t = group * GROUP + j
            c_now = c_ref[t, NSTATE:, :]
            for k in range(tiles):
                decay = jnp.exp2(rates[k] * spread(step_ref[group, j : j + 1, cols(k)]))
                states[k] = decay * (states[k] + c_now * spread(grad_ref[group, j : j + 1, cols(k)]))
        return tuple(states)

    start = tuple(jnp.zeros((NSTATE, LANES), jnp.float32) for _ in range(tiles))
    ends = lax.fori_loop(0, groups, body, start)
    for k in range(tiles):
        end_ref[:, cols(k)] = ends[k]


def forward_kernel(step_ref, flow_ref, bc_ref, rate_ref, enter_ref, out_ref):
    groups, unused, width = step_ref.shape
    tiles = width // LANES
    rates = [rate_ref[:, cols(k)] for k in range(tiles)]
    masks = fold_masks()

    def body(group, states):
        states = list(states)
        parts = [[] for _ in range(tiles)]
        for j in range(GROUP):
            t = group * GROUP + j
            b_now, c_now = bc_ref[t, :NSTATE, :], bc_ref[t, NSTATE:, :]
            for k in range(tiles):
                decay = jnp.exp2(rates[k] * spread(step_ref[group, j : j + 1, cols(k)]))
                states[k] = decay * states[k] + b_now * spread(flow_ref[group, j : j + 1, cols(k)])
                parts[k].append(halves(states[k] * c_now))
        for k in range(tiles):
            out_ref[group, :, cols(k)] = fold(parts[k], masks)
        return tuple(states)

    start = tuple(enter_ref[:, cols(k)] for k in range(tiles))
    lax.fori_loop(0, groups, body, start)


def reverse_kernel(
    held,
    step_ref,
    delta_ref,
    flow_ref,
    conv_ref,
    grad_ref,
    bc_ref,
    rate_ref,
    a_ref,
    enter_ref,
    leave_ref,
    *refs,
):
    gdelta_ref, gconv_ref, gbc_ref, ga_ref, decay_scr, state_scr = refs[held:]
    groups, unused, width = step_ref.shape
    tiles = width // LANES
    rates = [rate_ref[:, cols(k)] for k in range(tiles)]
    masks = fold_masks()

    def ahead(group, states):
        states = list(states)
        for j in range(GROUP):
            t = group * GROUP + j
            b_now = bc_ref[t, :NSTATE, :]
            for k in range(tiles):
                decay = jnp.exp2(rates[k] * spread(step_ref[group, j : j + 1, cols(k)]))
                state_scr[t, :, cols(k)] = states[k]
                decay_scr[t, :, cols(k)] = decay
                states[k] = decay * states[k] + b_now * spread(flow_ref[group, j : j + 1, cols(k)])
        return tuple(states)

    start = tuple(enter_ref[:, cols(k)] for k in range(tiles))
    ends = lax.fori_loop(0, groups, ahead, start)
    for k in range(tiles):
        state_scr[groups * GROUP, :, cols(k)] = ends[k]

    @pl.when(pl.program_id(0) == 0)
    def clear():
        gbc_ref[...] = jnp.zeros_like(gbc_ref)

    def back(lap, carried):
        carried, totals = list(carried[0]), list(carried[1])
        group = groups - 1 - lap
        inputs = [[] for _ in range(tiles)]
        drifts = [[] for _ in range(tiles)]
        for j in reversed(range(GROUP)):
            t = group * GROUP + j
            b_now, c_now = bc_ref[t, :NSTATE, :], bc_ref[t, NSTATE:, :]
            sum_b = sum_c = None
            for k in range(tiles):
                grad = spread(grad_ref[group, j : j + 1, cols(k)])
                flow = spread(flow_ref[group, j : j + 1, cols(k)])
                step = spread(delta_ref[group, j : j + 1, cols(k)])
                state_grad = carried[k] + grad * c_now
                inputs[k].insert(0, halves(state_grad * b_now))
                term_b = state_grad * flow
                term_c = state_scr[t + 1, :, cols(k)] * grad
                sum_b = term_b if sum_b is None else sum_b + term_b
                sum_c = term_c if sum_c is None else sum_c + term_c
                carried[k] = decay_scr[t, :, cols(k)] * state_grad
                term = carried[k] * state_scr[t, :, cols(k)]
                drifts[k].insert(0, halves(term * a_ref[:, cols(k)]))
                totals[k] = totals[k] + term * step
            gbc_ref[t, :NSTATE, :] = gbc_ref[t, :NSTATE, :] + sum_b
            gbc_ref[t, NSTATE:, :] = gbc_ref[t, NSTATE:, :] + sum_c
        for k in range(tiles):
            entry = fold(inputs[k], masks)
            gdelta_ref[group, :, cols(k)] = fold(drifts[k], masks) + entry * conv_ref[group, :, cols(k)]
            gconv_ref[group, :, cols(k)] = entry * delta_ref[group, :, cols(k)]
        return (tuple(carried), tuple(totals))

    start = tuple(leave_ref[:, cols(k)] for k in range(tiles))
    zeros = tuple(jnp.zeros((NSTATE, LANES), jnp.float32) for _ in range(tiles))
    unused, totals = lax.fori_loop(0, groups, back, (start, zeros))
    for k in range(tiles):
        ga_ref[:, cols(k)] = totals[k]


def row_spec(rows, width):
    return pl.BlockSpec((None, rows // GROUP, GROUP, width), lambda s, c: (s, 0, 0, c))


def grouped(*arrays):
    return tuple(a.reshape(a.shape[0], -1, GROUP, a.shape[-1]) for a in arrays)


def bc_spec(rows):
    return pl.BlockSpec((None, rows, 2 * NSTATE, LANES), lambda s, c: (s, 0, 0, 0))


def rate_spec(width):
    return pl.BlockSpec((NSTATE, width), lambda s, c: (0, c))


def state_spec(width):
    return pl.BlockSpec((None, NSTATE, width), lambda s, c: (s, 0, c))


def f32(*shape):
    return jax.ShapeDtypeStruct(shape, jnp.float32)


def limits(mb):
    return pltpu.CompilerParams(vmem_limit_bytes=mb * 2**20)


def forward_end(step, flow, bc, rate, width):
    seqs, rows, channels = step.shape
    return pl.pallas_call(
        forward_end_kernel,
        grid=(seqs, channels // width),
        in_specs=[row_spec(rows, width)] * 2 + [bc_spec(rows), rate_spec(width)],
        out_specs=state_spec(width),
        out_shape=f32(seqs, NSTATE, channels),
        compiler_params=limits(40),
        name="forward_end",
    )(*grouped(step, flow), bc, rate)


def reverse_end(step, grad, bc, rate, width):
    seqs, rows, channels = step.shape
    return pl.pallas_call(
        reverse_end_kernel,
        grid=(seqs, channels // width),
        in_specs=[row_spec(rows, width)] * 2 + [bc_spec(rows), rate_spec(width)],
        out_specs=state_spec(width),
        out_shape=f32(seqs, NSTATE, channels),
        compiler_params=limits(40),
        name="reverse_end",
    )(*grouped(step, grad), bc, rate)


def forward_main(step, flow, bc, rate, enter, width):
    seqs, rows, channels = step.shape
    return pl.pallas_call(
        forward_kernel,
        grid=(seqs, channels // width),
        in_specs=[row_spec(rows, width)] * 2 + [bc_spec(rows), rate_spec(width), state_spec(width)],
        out_specs=row_spec(rows, width),
        out_shape=f32(seqs, rows // GROUP, GROUP, channels),
        compiler_params=limits(40),
        name="forward_main",
    )(*grouped(step, flow), bc, rate, enter).reshape(step.shape)


def reverse_main(step, delta, flow, conv, grad, bc, rate, a_mat, enter, leave, width, seq, into=()):
    seqs, rows, channels = step.shape

    def of_seq(*block):
        return pl.BlockSpec((None,) + block, lambda c: (seq,) + (0,) * (len(block) - 1) + (c,))

    row = of_seq(rows // GROUP, GROUP, width)
    state = of_seq(NSTATE, width)
    pairs = pl.BlockSpec((None, rows, 2 * NSTATE, LANES), lambda c: (seq, 0, 0, 0))
    rates = pl.BlockSpec((NSTATE, width), lambda c: (0, c))
    return pl.pallas_call(
        functools.partial(reverse_kernel, len(into)),
        grid=(channels // width,),
        in_specs=[row] * 5
        + [pairs, rates, rates, state, state]
        + [pl.BlockSpec(memory_space=pl.ANY)] * len(into),
        out_specs=[row, row, pairs, state],
        out_shape=[f32(seqs, rows // GROUP, GROUP, channels)] * 2
        + [f32(seqs, rows, 2 * NSTATE, LANES), f32(seqs, NSTATE, channels)],
        input_output_aliases={10 + n: n for n in range(len(into))},
        scratch_shapes=[
            pltpu.VMEM((rows, NSTATE, width), jnp.float32),
            pltpu.VMEM((rows + 1, NSTATE, width), jnp.float32),
        ],
        compiler_params=limits(56),
        name="reverse_main",
    )(*grouped(step, delta, flow, conv, grad), bc, rate, a_mat, enter, leave, *into)


def place_of(piece):
    width = LANES
    return pl.ds(pl.multiple_of((lax.axis_index(DP) ^ piece) * width, width), width)


def piece_spec(n, width, piece=0):
    if n is None:
        return pl.BlockSpec((LANES, width), lambda j: (lax.axis_index(DP) ^ piece, j))
    return pl.BlockSpec((LANES, width), lambda j: (n, j))


def up_kernel(x_ref, *refs):
    pieces, out_ref, x_scr = refs[:-2], refs[-2], refs[-1]

    @pl.when(pl.program_id(0) == 0)
    def order():
        for p in range(len(pieces)):
            x_scr[:, cols(p)] = x_ref[:, place_of(p)]

    weights = jnp.concatenate([ref[...] for ref in pieces], axis=0)
    out_ref[...] = jnp.dot(x_scr[...], weights, preferred_element_type=jnp.float32).astype(
        out_ref.dtype
    )


def up(x, pieces, kind, width=512):
    rows, features = x.shape
    channels = pieces[0][0].shape[1]
    return pl.pallas_call(
        up_kernel,
        grid=(channels // width,),
        in_specs=[pl.BlockSpec((rows, features), lambda j: (0, 0))]
        + [piece_spec(n, width) for unused, n in pieces],
        out_specs=pl.BlockSpec((rows, width), lambda j: (0, j)),
        out_shape=jax.ShapeDtypeStruct((rows, channels), kind),
        scratch_shapes=[pltpu.VMEM((rows, features), x.dtype)],
        compiler_params=limits(40),
        name="up",
    )(x, *[array for array, unused in pieces])


def down_kernel(groups, *refs):
    inputs, pieces = refs[:groups], refs[groups:-3]
    own_ref, other_ref, total = refs[-3:]
    count = len(pieces) // groups
    new = None
    for g, y_ref in enumerate(inputs):
        weights = jnp.concatenate([ref[...] for ref in pieces[g * count : (g + 1) * count]], axis=0)
        term = lax.dot_general(
            y_ref[...], weights, (((1,), (1,)), ((), ())), preferred_element_type=jnp.float32
        )
        new = term if new is None else new + term

    @pl.when(pl.program_id(0) == 0)
    def first():
        total[...] = new

    @pl.when(pl.program_id(0) > 0)
    def later():
        total[...] += new

    @pl.when(pl.program_id(0) == pl.num_programs(0) - 1)
    def last():
        half = count // 2
        mine = lax.axis_index(TENSOR) * half
        for r in range(half):
            own_ref[:, cols(r)] = total[:, place_of(mine + r)]
            other_ref[:, cols(r)] = total[:, place_of((half - mine) + r)].astype(other_ref.dtype)


def down(pairs, kind, width=512):
    rows, channels = pairs[0][0].shape
    count = len(pairs[0][1])
    features = count * LANES
    half = pl.BlockSpec((rows, features // 2), lambda j: (0, 0))
    return pl.pallas_call(
        functools.partial(down_kernel, len(pairs)),
        grid=(channels // width,),
        in_specs=[pl.BlockSpec((rows, width), lambda j: (0, j))] * len(pairs)
        + [
            piece_spec(n, width, piece)
            for unused, pieces in pairs
            for piece, (array, n) in enumerate(pieces)
        ],
        out_specs=[half, half],
        out_shape=[
            jax.ShapeDtypeStruct((rows, features // 2), jnp.float32),
            jax.ShapeDtypeStruct((rows, features // 2), kind),
        ],
        scratch_shapes=[pltpu.VMEM((rows, features), jnp.float32)],
        compiler_params=limits(48),
        name="down",
    )(*[y for y, unused in pairs], *[array for unused, pieces in pairs for array, n in pieces])


def outer_kernel(x_ref, y_ref, *refs):
    outs, x_scr = refs[:-1], refs[-1]

    @pl.when(pl.program_id(0) == 0)
    def order():
        for p in range(x_ref.shape[1] // LANES):
            part = x_ref[:, place_of(p)].astype(jnp.float32)
            x_scr[pl.ds(p * LANES, LANES), :] = part.T.astype(x_scr.dtype)

    product = jnp.dot(x_scr[...], y_ref[...], preferred_element_type=jnp.float32)
    for p in range(product.shape[0] // LANES):
        row = (0, 2, 1, 3)[p // len(outs)] * LANES
        part = product[p * LANES : (p + 1) * LANES]
        outs[p % len(outs)][row : row + LANES, :] = part.astype(outs[0].dtype)


def outer(x, y, width=512):
    rows, features = x.shape
    channels = y.shape[1]
    stacked = features // 4
    return pl.pallas_call(
        outer_kernel,
        grid=(channels // width,),
        in_specs=[
            pl.BlockSpec((rows, features), lambda j: (0, 0)),
            pl.BlockSpec((rows, width), lambda j: (0, j)),
        ],
        out_specs=[pl.BlockSpec((stacked, width), lambda j: (0, j))] * 4,
        out_shape=[jax.ShapeDtypeStruct((stacked, channels), jnp.bfloat16)] * 4,
        scratch_shapes=[pltpu.VMEM((features, rows), x.dtype)],
        compiler_params=limits(48),
        name="outer",
    )(x, y)


def assemble_kernel(blocks, extra_ref, proj_ref, rest_ref, dt_ref):
    depth = dt_ref.shape[0] // (dt_ref.shape[1] // LANES)
    proj_blocks = proj_ref.shape[0] // NSTATE
    odd = lax.rem(lax.axis_index(DP), 2) == 1
    for p in range(0, 16, 2):
        slot = (p >> 2) + (p & 2) * 2
        for core in range(2):
            here = place_of(p + core)
            for b in range(blocks):
                block = extra_ref[core, slot, :NSTATE, cols(b)]
                row = (b if b < proj_blocks else b - proj_blocks) * NSTATE
                if b < proj_blocks:
                    proj_ref[row : row + NSTATE, here] = block
                else:
                    rest_ref[row : row + NSTATE, here] = block.astype(jnp.float32)
        own = extra_ref[0, slot, NSTATE:, :].astype(jnp.float32)[:depth]
        other = extra_ref[1, slot, NSTATE:, :].astype(jnp.float32)[:depth]
        pair = jnp.concatenate(
            [jnp.where(odd, other, own), jnp.where(odd, own, other)], axis=0
        ).astype(dt_ref.dtype)
        first = (lax.axis_index(DP) ^ p) // 2
        dt_ref[pl.ds(pl.multiple_of(first * 2 * depth, 2 * depth), 2 * depth), :] = pair


def assemble(extra, proj_rows, rest_rows):
    channels = extra.shape[-1]
    return pl.pallas_call(
        functools.partial(assemble_kernel, (proj_rows + rest_rows) // NSTATE),
        out_shape=[
            jax.ShapeDtypeStruct((proj_rows, channels), extra.dtype),
            f32(rest_rows, channels),
            jax.ShapeDtypeStruct((RANK, channels), extra.dtype),
        ],
        compiler_params=limits(40),
        name="assemble",
    )(extra)


def deal_kernel(proj_ref, dt_ref, rest_ref, out_ref):
    count = out_ref.shape[0]
    bits = count.bit_length() - 1
    depth = dt_ref.shape[0] // count
    proj_rows = proj_ref.shape[0]
    rest_row = proj_rows + dt_ref.shape[0]
    for n in range(count):
        piece = sum(1 << (bits - 1 - b) for b in range(bits) if n >> b & 1)
        out_ref[n, :proj_rows, :] = proj_ref[:, place_of(piece)].astype(out_ref.dtype)
        out_ref[n, rest_row:, :] = rest_ref[:, place_of(piece)].astype(out_ref.dtype)
        place = pl.ds(pl.multiple_of((lax.axis_index(DP) ^ piece) * depth, depth), depth)
        for k in range(0, count, 2):
            both = jnp.concatenate([dt_ref[place, cols(k)], dt_ref[place, cols(k + 1)]], axis=0)
            row = proj_rows + k * depth
            out_ref[n, row : row + 2 * depth, :] = both.astype(out_ref.dtype)


def deal(proj, dt, rest):
    rows = proj.shape[0] + dt.shape[0] + rest.shape[0]
    return pl.pallas_call(
        deal_kernel,
        out_shape=jax.ShapeDtypeStruct((proj.shape[1] // LANES, rows, LANES), jnp.bfloat16),
        compiler_params=limits(40),
        name="deal",
    )(proj, dt, rest)


EPSILON = 1e-05
RESET = 1e30


def shifted(block, axis, distance):
    devices = range(lax.axis_size(axis))
    route = [(i - distance, i) for i in devices if i - distance in devices]
    return lax.ppermute(block, axis, route)


def swapped(block, axis):
    return lax.ppermute(block, axis, [(0, 1), (1, 0)])


def exchanged(block, mask):
    return lax.ppermute(block, DP, [(i, i ^ mask) for i in range(lax.axis_size(DP))])


def after(block, *earlier):
    return lax.optimization_barrier((block, *earlier))[0] if earlier else block


def sent(block, mask, name, *earlier):
    with jax.named_scope(f"{name}_to_{mask}"):
        return exchanged(after(block, *earlier), mask)


def round_masks():
    return [1 << n for n in range(lax.axis_size(DP).bit_length() - 1)]


def total(*blocks):
    result = blocks[0].astype(jnp.float32)
    for block in blocks[1:]:
        result = result + block.astype(jnp.float32)
    return result


def silu_slope(values):
    squash = jax.nn.sigmoid(values)
    return squash * (1.0 + values * (1.0 - squash))


def dot(left, right, dims):
    return lax.dot_general(left, right, (dims, ((), ())), preferred_element_type=jnp.float32)


def joined(block, axis):
    if lax.axis_size(axis) != 2:
        return lax.all_gather(block, axis, axis=block.ndim - 1, tiled=True)
    other = swapped(block, axis)
    first = lax.axis_index(axis) == 0
    return jnp.concatenate(
        [jnp.where(first, block, other), jnp.where(first, other, block)], axis=-1
    )


def summed(block, axis):
    if lax.axis_size(axis) != 2:
        return lax.psum(block, axis)
    return block + swapped(block, axis)


def sum_scattered(block, axis):
    last = block.ndim - 1
    if lax.axis_size(axis) != 2:
        return lax.psum_scatter(block, axis, scatter_dimension=last, tiled=True)
    width = block.shape[-1] // 2
    place = lax.axis_index(axis)
    own = lax.dynamic_slice_in_dim(block, place * width, width, last)
    other = lax.dynamic_slice_in_dim(block, (1 - place) * width, width, last)
    return own + swapped(other, axis)


def entering(value, span, rate, axis, direction):
    value = shifted(value, axis, direction)
    span = shifted(span, axis, direction)
    distance = 1
    while distance < lax.axis_size(axis):
        further = shifted(value, axis, direction * distance)
        further_span = shifted(span, axis, direction * distance)
        value = value + jnp.exp2(rate[None] * span[:, None, :]) * further
        span = span + further_span
        distance *= 2
    return value


def local_whole(
    tokens, segments, cotangent, norm_gain, w_in, conv_w, conv_b, w_x, w_dt, dt_bias, a_log, d_skip, w_out
):
    seqs, rows, part = tokens.shape
    features, channels = part * lax.axis_size(TENSOR), w_in.shape[2]
    devices = lax.axis_size(DP)
    shard = channels // devices
    taps = conv_w.shape[0]
    reach = taps - 1
    block = min(512, channels)
    count = seqs * rows
    low = jnp.bfloat16

    small = jnp.concatenate(
        [
            conv_w,
            conv_b[None],
            dt_bias[None],
            d_skip[None],
            a_log.T,
            w_x.T,
            w_dt.reshape(-1, shard),
            norm_gain.reshape(-1, shard),
        ],
        axis=0,
    )
    small = lax.all_gather(small, DP)
    w_in_x = lax.all_gather(w_in[:, 0], DP, axis=0, tiled=True)
    w_in_gate = lax.all_gather(w_in[:, 1], DP, axis=0, tiled=True)
    w_out_t = lax.all_gather(w_out.T, DP, axis=0, tiled=True)
    channel_rows = taps + 3 + NSTATE + w_x.shape[1]
    by_channel = small[:, :channel_rows].transpose(1, 0, 2).reshape(channel_rows, channels)
    taps_f = by_channel[:taps].astype(jnp.float32)
    bias_f, shift_f, skip_f = (by_channel[taps + i].astype(jnp.float32)[None] for i in range(3))
    a_mat = -jnp.exp(by_channel[taps + 3 : taps + 3 + NSTATE].astype(jnp.float32))
    rate = a_mat * LOG2E
    w_x_t = by_channel[taps + 3 + NSTATE :]
    dt_full = small[:, channel_rows : channel_rows + RANK].reshape(RANK, channels)
    gain_f = small[:, channel_rows + RANK :].reshape(features).astype(jnp.float32)

    marks_own = segments + 1
    marks_before = shifted(marks_own[:, rows - reach :], DP, 1)
    marks = jnp.concatenate([marks_before, marks_own], axis=1)
    tail = shifted(tokens[:, rows - reach :], DP, 1)
    wanted = jnp.concatenate(
        [tokens.reshape(count, part), tail.reshape(seqs * reach, part)], axis=0
    )
    x_rows = joined(wanted, TENSOR).astype(jnp.float32)
    cot = joined(cotangent.reshape(count, part), TENSOR)
    scale_all = lax.rsqrt(jnp.mean(x_rows * x_rows, axis=1, keepdims=True) + EPSILON)
    normed_all = (x_rows * scale_all * gain_f[None]).astype(low)
    normed, scale = normed_all[:count], scale_all[:count]

    inner_all = dot(normed_all, w_in_x, ((1,), (0,))).astype(low)
    inner_ext = jnp.concatenate(
        [
            inner_all[count:].reshape(seqs, reach, channels),
            inner_all[:count].reshape(seqs, rows, channels),
        ],
        axis=1,
    ).astype(jnp.float32)
    tap_masks = [
        (marks[:, k : k + rows] == marks_own).astype(jnp.float32)[:, :, None] for k in range(taps)
    ]
    mixed = bias_f[None]
    for k in range(taps):
        mixed = mixed + taps_f[k][None, None] * inner_ext[:, k : k + rows] * tap_masks[k]
    conv_low = jax.nn.silu(mixed).astype(low)
    conv = conv_low.astype(jnp.float32)
    conv_flat = conv_low.reshape(count, channels)
    proj = summed(dot(conv_flat, w_x_t, ((1,), (1,))), TENSOR)
    rank_part = proj[:, :RANK].astype(low)
    bc = jnp.broadcast_to(
        proj[:, RANK:].reshape(seqs, rows, 2 * NSTATE, 1), (seqs, rows, 2 * NSTATE, LANES)
    )
    pre = (dot(rank_part, dt_full, ((1,), (0,))) + shift_f).reshape(seqs, rows, channels)
    delta = jax.nn.softplus(pre)
    step = jnp.where(tap_masks[reach - 1] > 0, delta, RESET)
    flow = delta * conv
    span = jnp.sum(step, axis=1)

    end = forward_end(step, flow, bc, rate, block)
    enter = entering(end, span, rate, DP, 1)
    readout = forward_main(step, flow, bc, rate, enter, block)
    ssm = readout + skip_f[None] * conv

    gate = dot(normed, w_in_gate, ((1,), (0,))).reshape(seqs, rows, channels)
    silu_gate = jax.nn.silu(gate)
    gated = (ssm * silu_gate).astype(low).reshape(count, channels)
    branch = sum_scattered(dot(gated, w_out_t, ((1,), (1,))), TENSOR)
    tokens_f = tokens.reshape(count, part).astype(jnp.float32)
    block_out = (tokens_f + branch).astype(low).reshape(seqs, rows, part)
    grad_out_t = dot(cot, gated, ((0,), (0,))).astype(low)
    grad_out_t = lax.psum_scatter(grad_out_t, DP, scatter_dimension=0, tiled=True)
    grad_gated = dot(cot, w_out_t, ((1,), (0,))).reshape(seqs, rows, channels)
    grad_ssm = grad_gated * silu_gate
    grad_gate = (grad_gated * ssm * silu_slope(gate)).astype(low).reshape(count, channels)
    grad_in_gate = dot(normed, grad_gate, ((0,), (0,))).astype(low)
    grad_in_gate = lax.psum_scatter(grad_in_gate, DP, scatter_dimension=0, tiled=True)
    grad_skip = jnp.sum(grad_ssm * conv, axis=(0, 1))

    back_end = reverse_end(step, grad_ssm, bc, rate, block)
    leave = entering(back_end, span, rate, DP, -1)
    back = ()
    for n in range(seqs):
        back = reverse_main(
            step, delta, flow, conv, grad_ssm, bc, rate, a_mat, enter, leave, block, n, back
        )
    grad_delta, grad_conv_scan, grad_bc, grad_a = back
    grad_delta, grad_conv_scan = (part.reshape(step.shape) for part in (grad_delta, grad_conv_scan))
    grad_alog = jnp.sum(grad_a, axis=0) * a_mat
    grad_pre = grad_delta * jax.nn.sigmoid(pre)
    grad_shift = jnp.sum(grad_pre, axis=(0, 1))
    grad_pre_low = grad_pre.astype(low).reshape(count, channels)
    grad_dt = dot(rank_part, grad_pre_low, ((0,), (0,)))
    grad_rank = dot(grad_pre_low, dt_full, ((1,), (1,)))
    grad_proj = jnp.concatenate(
        [grad_rank, jnp.sum(grad_bc, axis=-1).reshape(count, 2 * NSTATE)], axis=1
    )
    grad_proj = summed(grad_proj, TENSOR).astype(low)
    grad_x_t = dot(grad_proj, conv_flat, ((0,), (0,)))
    grad_conv = (
        grad_conv_scan
        + skip_f[None] * grad_ssm
        + dot(grad_proj, w_x_t, ((1,), (0,))).reshape(seqs, rows, channels)
    )
    grad_mixed = grad_conv * silu_slope(mixed)
    grad_bias = jnp.sum(grad_mixed, axis=(0, 1))
    grad_taps = jnp.stack(
        [
            jnp.sum(grad_mixed * inner_ext[:, k : k + rows] * tap_masks[k], axis=(0, 1))
            for k in range(taps)
        ]
    )
    grad_ext = jnp.zeros((seqs, rows + reach, channels), jnp.float32)
    for k in range(taps):
        grad_ext = grad_ext + jnp.pad(
            taps_f[k][None, None] * grad_mixed * tap_masks[k], ((0, 0), (k, reach - k), (0, 0))
        )
    returned = shifted(grad_ext[:, :reach], DP, -1)
    grad_inner = grad_ext[:, reach:] + jnp.pad(returned, ((0, 0), (rows - reach, 0), (0, 0)))
    grad_inner = grad_inner.astype(low).reshape(count, channels)
    grad_in_x = dot(normed, grad_inner, ((0,), (0,))).astype(low)
    grad_in_x = lax.psum_scatter(grad_in_x, DP, scatter_dimension=0, tiled=True)

    grad_normed = sum_scattered(
        dot(grad_inner, w_in_x, ((1,), (1,))) + dot(grad_gate, w_in_gate, ((1,), (1,))), TENSOR
    )
    column = lax.axis_index(TENSOR) * part
    gain_local = lax.dynamic_slice_in_dim(gain_f, column, part, 0)
    weighted = grad_normed * gain_local[None]
    grad_gain = jnp.sum(grad_normed * tokens_f * scale, axis=0)
    grad_gain = lax.dynamic_update_slice_in_dim(
        jnp.zeros((features,), jnp.float32), grad_gain, column, 0
    )
    row_total = summed(jnp.sum(weighted * tokens_f, axis=1, keepdims=True), TENSOR)
    input_grad = (
        cotangent.reshape(count, part).astype(jnp.float32)
        + scale * weighted
        - tokens_f * (scale * scale * scale) * (row_total / features)
    ).reshape(seqs, rows, part)

    by_channel = jnp.concatenate(
        [grad_taps, grad_bias[None], grad_shift[None], grad_skip[None], grad_alog, grad_x_t], axis=0
    )
    by_channel = by_channel.reshape(channel_rows, devices, shard).transpose(1, 0, 2)
    packed = jnp.concatenate(
        [
            by_channel,
            grad_dt.reshape(devices, RANK, shard),
            grad_gain.reshape(devices, -1, shard),
        ],
        axis=1,
    )
    packed = lax.psum_scatter(packed, DP, scatter_dimension=0)
    by_channel = packed[:channel_rows]
    grad_dt = packed[channel_rows : channel_rows + RANK].reshape(-1, channels)
    grad_gain = summed(packed[channel_rows + RANK :], TENSOR).reshape(-1)
    grad_in = jnp.stack([grad_in_x, grad_in_gate], axis=1).astype(jnp.float32)
    return (
        block_out,
        input_grad,
        grad_gain,
        grad_in,
        by_channel[:taps],
        by_channel[taps],
        by_channel[taps + 3 + NSTATE :].T,
        grad_dt,
        by_channel[taps + 1],
        by_channel[taps + 3 : taps + 3 + NSTATE].T,
        by_channel[taps + 2],
        grad_out_t.astype(jnp.float32).T,
    )


class Names:
    def __getattr__(self, name):
        return name


N = Names()


class Plan:
    def __init__(self, waits):
        self.waits, self.steps, self.values, self.open = waits, {}, {}, set()

    def add(self, name, step):
        self.steps[name] = step

    def get(self, name):
        if name not in self.values:
            if name in self.open:
                raise ValueError(f"cycle at {name}")
            self.open.add(name)
            self.values[name] = self.steps[name]()
            self.open.remove(name)
        return self.values[name]

    def first(self, name):
        value = self.get(name)
        return value[0] if isinstance(value, (tuple, list)) else value

    def tied(self, name, block):
        return after(block, *(self.first(other) for other in self.waits.get(name, ())))

    def send(self, name, block, mask):
        def step():
            with jax.named_scope(name):
                return exchanged(self.tied(name, block()), mask)

        self.add(name, step)

    def swap(self, name, block):
        def step():
            with jax.named_scope(name):
                return swapped(self.tied(name, block()), TENSOR)

        self.add(name, step)


def gather_steps(plan, chunk, shard, groups, rows):
    places = {}

    def block(pieces):
        parts = []
        for n, piece in enumerate(pieces):
            name, row = places[piece]
            array = plan.get(name) if name else shard()
            part = array[row * LANES : row * LANES + rows] if array.shape[0] != rows else array
            parts.append(part)
        return parts[0] if len(parts) == 1 else jnp.concatenate(parts, axis=0)

    def move(name, pieces, mask):
        def start():
            return block(pieces)

        plan.send(name, start, mask)
        for n, piece in enumerate(pieces):
            places[piece + mask] = (name, n)

    places[0] = (None, 0)
    move(f"{chunk}4", (0,), 4)
    move(f"{chunk}8", (0,), 8)
    move(f"{chunk}12", (8,), 4)
    for group in groups:
        move(f"{chunk}x{group[0]}", group, 2)

    def core(name, pieces):
        first, *others = (block((p,))[:LANES] for p in pieces)
        return jnp.concatenate([plan.tied(name, first), *others], axis=0)

    for x in (0, 2):
        name, pieces = f"{chunk}s{x}", [z + x for z in (0, 4, 8, 12)]
        plan.send(name, lambda name=name, pieces=pieces: core(name, pieces), 1)
        for n, piece in enumerate(pieces):
            places[piece + 1] = (name, n)

    def pieces():
        return [(plan.get(places[p][0]) if places[p][0] else shard(), places[p][1]) for p in range(16)]

    def extra():
        return jnp.stack([block((p,))[LANES:] for p in (0, 4, 8, 12, 2, 6, 10, 14)])

    plan.add(chunk, pieces)
    if rows > LANES:
        plan.add(f"{chunk}own", extra)
        plan.send(f"{chunk}e", lambda: plan.get(f"{chunk}own"), 1)


ROWS = {0: 0, 8: 1, 4: 2, 12: 3}


def scatter_steps(plan, name, outer_name, groups, near_groups):
    crossed, neared = {}, {}

    def rows_of(group):
        first = ROWS[group[0]]
        return slice(first * LANES, (first + len(group)) * LANES)

    def chip(x, group):
        return [plan.get(outer_name)[x][rows_of(group)], plan.get(f"{name}s{x}")[rows_of(group)]]

    def pick(table, z):
        step, n = table[z]
        return plan.get(step)[n * LANES : (n + 1) * LANES]

    for x in (2, 0):
        plan.send(f"{name}s{x}", lambda x=x: plan.get(outer_name)[x + 1], 1)
    for group in groups:
        ready, step = f"{name}p{group[0]}", f"{name}x{group[0]}"
        plan.add(ready, lambda group=group: total(*chip(2, group)).astype(jnp.bfloat16))
        plan.send(step, lambda ready=ready: plan.get(ready), 2)
        for n, z in enumerate(group):
            crossed[z] = (step, n)

    def column(group):
        parts = [
            total(*chip(0, (z,)), pick(crossed, z), *([pick(neared, z)] if z == 8 else [])) for z in group
        ]
        return jnp.concatenate(parts, axis=0).astype(jnp.bfloat16)

    for group in near_groups:
        step = f"{name}z{group[0]}"
        plan.send(step, lambda group=group: column(group), 4)
        for n, z in enumerate(group):
            neared[z - 4] = (step, n)
    plan.send(f"{name}z8", lambda: column((8,)), 8)

    def result():
        last = plan.tied(name, plan.get(f"{name}z8"))
        return total(last, pick(neared, 0), pick(crossed, 0), *chip(0, (0,)))

    plan.add(name, result)


def state_steps(plan, name, value, span, rate, known=None):
    low = jnp.bfloat16

    def message(n):
        mask = round_masks()[n]
        lower = lax.rem(lax.div(lax.axis_index(DP), mask), 2) == 0
        now = plan.get(f"{name}in{n}")
        got = plan.get(f"{name}{n}")
        other = got[:, :NSTATE].astype(jnp.float32)
        own_span, other_span, before, behind = plan.get(f"{known or name}spans{n}")
        first = ~lower if known else lower
        far = jnp.where(first, 0.0, other)
        decay = lambda steps: jnp.exp2(rate()[None] * steps[:, None, :])
        result = far if n == 0 else now[1] + decay(behind if known else before) * far
        through = jnp.where(first, other_span, own_span)
        value = jnp.where(first, other, now[0]) + decay(through) * jnp.where(first, now[0], other)
        return value, result

    def spans(n):
        if n == 0:
            own, before, behind = span(), jnp.zeros_like(span()), jnp.zeros_like(span())
        else:
            own, other, before, behind = plan.get(f"{name}spans{n - 1}")
            lower = lax.rem(lax.div(lax.axis_index(DP), round_masks()[n - 1]), 2) == 0
            before = before + jnp.where(lower, 0.0, other)
            behind = behind + jnp.where(lower, other, 0.0)
            own = own + other
        with jax.named_scope(f"{name}span{n}"):
            other = exchanged(plan.tied(f"{name}span{n}", own), round_masks()[n])
        return own, other, before, behind

    count = len(round_masks())
    for n in range(count):
        plan.add(f"{name}in{n}", lambda n=n: message(n - 1) if n else (value(), None))
        plan.send(f"{name}{n}", lambda n=n: plan.get(f"{name}in{n}")[0].astype(low), round_masks()[n])
        if not known:
            plan.add(f"{name}spans{n}", lambda n=n: spans(n))
    plan.add(name, lambda: message(count - 1)[1])


def pack_steps(plan, name, blocks):
    def sums(n):
        if n == 0:
            return blocks()
        before = sums_of(n - 1)
        half = before.shape[0] // 2
        return before[:half].astype(jnp.float32) + plan.get(f"{name}{n - 1}").astype(jnp.float32)

    def sums_of(n):
        return plan.get(f"{name}sum{n}")

    def sent_half(n):
        block = sums_of(n)
        return block[block.shape[0] // 2 :].astype(jnp.bfloat16)

    for n in range(len(round_masks()) + 1):
        plan.add(f"{name}sum{n}", lambda n=n: sums(n))
    for n, mask in enumerate(round_masks()):
        plan.send(f"{name}{n}", lambda n=n: sent_half(n), mask)
    plan.add(name, lambda: sums_of(len(round_masks()))[0])


WAITS = dict(
    a12=(N.a4, N.a8, N.ax0, N.bx0),
    ax4=(N.a4, N.a8, N.ax0, N.bx0),
    ax8=(N.a4, N.a8, N.ax0, N.bx0),
    b4=(N.a12,),
    b8=(N.a12,),
    ax12=(N.ax4, N.ax8, N.a12),
    as0=(N.ax4, N.ax8, N.a12),
    as2=(N.b4, N.b8),
    bx4=(N.as0, N.as2, N.ae),
    b12=(N.inner,),
    bx12=(N.f1,),
    bs0=(N.f1,),
    gate=(N.readout,),
    outB=(N.r0,),
    branch=(N.outB,),
    back0=(N.branch,),
    taps=(N.grad_normed,),
    c=(N.inner,),
    grad_gated=(N.outC,),
    back1=(N.Bx4,),
    grad_mixed=(N.Bx0, N.Bz12, N.yb),
    Bz8=(N.Ap4,),
    down=(N.Ap4, N.As0),
    Ax0=(N.Ap4,),
    yn=(N.Ax4, N.Bz8),
    y0=(N.ax0,),
    bs2=(N.readout,),
    grad_pre=(N.Bx4,),
    Az12=(N.As0,),
    ae=(N.ax8,),
)
GROUPS = dict(
    a=((0,), (4,), (8,), (12,)),
    b=((0,), (4,), (8,), (12,)),
    c=(),
    C=(),
    B=((4, 12), (0, 8)),
    A=((4, 12), (0, 8)),
    Cz=(),
    Bz=((12,), (4,)),
    Az=((12,), (4,)),
)


def local(
    tokens, segments, cotangent, norm_gain, w_in, conv_w, conv_b, w_x, w_dt, dt_bias, a_log, d_skip, w_out
):
    seqs, rows, part = tokens.shape
    features, channels = part * 2, w_in.shape[2]
    devices = lax.axis_size(DP)
    shard = channels // devices
    taps = conv_w.shape[0]
    reach = taps - 1
    block = min(512, channels)
    count = seqs * rows
    low = jnp.bfloat16
    plan = Plan(WAITS)
    get, add, tied = plan.get, plan.add, plan.tied
    first_half = lax.axis_index(TENSOR) == 0

    def natural(own, other):
        return jnp.concatenate(
            [jnp.where(first_half, own, other), jnp.where(first_half, other, own)], axis=-1
        )

    def up_any(x, weights):
        if isinstance(weights, list):
            return up(x, weights, jnp.float32)
        return dot(x, weights, ((1,), (0,)))

    def pieces_of(weights):
        return weights if isinstance(weights, list) else [(weights, None)] * devices

    proj_rows = w_x.shape[1]
    small = jnp.concatenate(
        [
            w_x.T,
            a_log.T,
            conv_w,
            conv_b[None],
            dt_bias[None],
            d_skip[None],
            norm_gain.reshape(-1, shard),
        ],
        axis=0,
    )
    rest_rows = small.shape[0] - proj_rows
    rest_rows += -rest_rows % NSTATE
    small = jnp.pad(small, ((0, channels // LANES * NSTATE - small.shape[0]), (0, 0)))
    small = small.reshape(-1, NSTATE, LANES).transpose(1, 0, 2).reshape(NSTATE, channels)
    steps = jnp.pad(w_dt, ((0, NSTATE - w_dt.shape[0]), (0, 0)))
    shard_x = jnp.concatenate([w_in[:, 0], small, steps], axis=0)
    shard_gate, shard_out = w_in[:, 1], w_out.T
    gather_steps(plan, N.a, lambda: shard_x, GROUPS[N.a], shard_x.shape[0])
    for name, held in ((N.b, shard_gate), (N.c, shard_out)):
        if GROUPS[name]:
            gather_steps(plan, name, lambda held=held: held, GROUPS[name], LANES)
        else:
            add(name, lambda name=name, held=held: lax.all_gather(tied(name, held), DP, axis=0, tiled=True))

    def small_weights():
        extra = jnp.stack([get(N.aown), get(N.ae)])
        w_x_t, rest, dt_full = assemble(tied(N.small, extra), proj_rows, rest_rows)
        a_mat = -jnp.exp(rest[:NSTATE])
        gain = rest[NSTATE + taps + 3]
        others = [rest[NSTATE + taps + i][None] for i in range(3)]
        return w_x_t, dt_full, a_mat, a_mat * LOG2E, rest[NSTATE : NSTATE + taps], gain, *others

    add(N.small, small_weights)

    marks_own = segments + 1
    marks_before = shifted(marks_own[:, rows - reach :], DP, 1)
    marks = jnp.concatenate([marks_before, marks_own], axis=1)
    tap_masks = [
        (marks[:, k : k + rows] == marks_own).astype(jnp.float32)[:, :, None] for k in range(taps)
    ]
    tail = shifted(tokens[:, rows - reach :], DP, 1)
    wanted = [cotangent.reshape(count, part), tokens.reshape(count, part)]
    wanted.append(tail.reshape(seqs * reach, part))
    wanted = jnp.concatenate(wanted, axis=0)
    wanted = jnp.pad(wanted, ((0, -wanted.shape[0] % 16), (0, 0)))
    tokens_f = tokens.reshape(count, part).astype(jnp.float32)
    plan.swap(N.y0, lambda: wanted)
    add(N.rows, lambda: natural(wanted, get(N.y0)))

    def normed():
        x_rows = get(N.rows)[count:].astype(jnp.float32)
        scale = lax.rsqrt(jnp.mean(x_rows * x_rows, axis=1, keepdims=True) + EPSILON)
        return (x_rows * scale * get(N.small)[5][None]).astype(low), scale

    add(N.normed, normed)
    add(N.cot, lambda: get(N.rows)[:count])

    add(N.inner, lambda: up(tied(N.inner, get(N.normed)[0]), get(N.a), low))

    def extended():
        inner = get(N.inner)
        before = inner[count : count + seqs * reach].reshape(seqs, reach, channels)
        now = inner[:count].reshape(seqs, rows, channels)
        return jnp.concatenate([before, now], axis=1).astype(jnp.float32)

    add(N.extended, extended)

    def mixed():
        taps_f, bias_f = get(N.small)[4], get(N.small)[6]
        result = bias_f[None]
        for k in range(taps):
            result = result + taps_f[k][None, None] * get(N.extended)[:, k : k + rows] * tap_masks[k]
        return result

    add(N.mixed, mixed)
    add(N.conv, lambda: jax.nn.silu(get(N.mixed)).astype(low))
    add(N.conv_flat, lambda: get(N.conv).reshape(count, channels))
    add(N.part, lambda: dot(get(N.conv_flat), get(N.small)[0], ((1,), (1,))))
    plan.swap(N.yp, lambda: get(N.part))
    add(N.proj, lambda: get(N.part) + get(N.yp))
    add(N.rank, lambda: get(N.proj)[:, :RANK].astype(low))

    def broadcast():
        columns = get(N.proj)[:, RANK:].reshape(seqs, rows, 2 * NSTATE, 1)
        return jnp.broadcast_to(columns, (seqs, rows, 2 * NSTATE, LANES))

    add(N.bc, broadcast)

    def pre():
        product = dot(get(N.rank), get(N.small)[1], ((1,), (0,)))
        return (product + get(N.small)[7]).reshape(seqs, rows, channels)

    add(N.pre, pre)
    add(N.delta, lambda: jax.nn.softplus(get(N.pre)))
    add(N.step, lambda: jnp.where(tap_masks[reach - 1] > 0, get(N.delta), RESET))
    add(N.flow, lambda: get(N.delta) * get(N.conv).astype(jnp.float32))
    add(N.span, lambda: jnp.sum(get(N.step), axis=1))

    def rate():
        return get(N.small)[3]

    add(N.end, lambda: forward_end(get(N.step), tied(N.end, get(N.flow)), get(N.bc), rate(), block))
    state_steps(plan, N.f, lambda: get(N.end), lambda: get(N.span), rate)
    add(N.enter, lambda: get(N.f))
    add(
        N.readout,
        lambda: forward_main(
            get(N.step), get(N.flow), get(N.bc), rate(), tied(N.readout, get(N.enter)), block
        ),
    )
    add(N.ssm, lambda: get(N.readout) + get(N.small)[8][None] * get(N.conv).astype(jnp.float32))

    def gate():
        own = tied(N.gate, get(N.normed)[0][:count])
        return up_any(own, get(N.b)).reshape(seqs, rows, channels)

    add(N.gate, gate)
    add(N.silu_gate, lambda: jax.nn.silu(get(N.gate)))
    add(N.gated, lambda: (get(N.ssm) * get(N.silu_gate)).astype(low).reshape(count, channels))
    def scatter(name, x, y, groups, near):
        if groups:
            add(f"out{name}", lambda: outer(x(), y()))
            scatter_steps(plan, name, f"out{name}", groups, near)
        else:
            add(f"out{name}", lambda: dot(x(), y(), ((0,), (0,))).astype(low))
            add(
                f"{name}rs",
                lambda: lax.psum_scatter(
                    tied(f"{name}rs", get(f"out{name}")), DP, scatter_dimension=0, tiled=True
                ),
            )
            add(name, lambda: tied(name, get(f"{name}rs")).astype(jnp.float32))

    scatter(N.C, lambda: get(N.cot), lambda: tied(N.outC, get(N.gated)), GROUPS[N.C], GROUPS[N.Cz])
    add(N.grad_gated, lambda: up_any(tied(N.grad_gated, get(N.cot)), get(N.c)))
    add(N.grad_gated3, lambda: get(N.grad_gated).reshape(seqs, rows, channels))
    add(N.grad_ssm, lambda: tied(N.grad_ssm, get(N.grad_gated3)) * get(N.silu_gate))

    def grad_gate():
        slope = silu_slope(get(N.gate))
        result = tied(N.grad_gate, get(N.grad_gated3)) * get(N.ssm) * slope
        return result.astype(low).reshape(count, channels)

    add(N.grad_gate, grad_gate)

    add(
        N.rend,
        lambda: reverse_end(get(N.step), tied(N.rend, get(N.grad_ssm)), get(N.bc), rate(), block),
    )
    state_steps(plan, N.r, lambda: get(N.rend), None, rate, N.f)
    scatter(N.B, lambda: get(N.normed)[0][:count], lambda: tied(N.outB, get(N.grad_gate)), GROUPS[N.B], GROUPS[N.Bz])
    add(N.branch, lambda: down([(tied(N.branch, get(N.gated)), pieces_of(get(N.c)))], low))
    plan.swap(N.yb, lambda: get(N.branch)[1])

    def back(n):
        into = get(f"back{n - 1}") if n else ()
        leave = tied(f"back{n}", get(N.r))
        inputs = [get(N.step), get(N.delta), get(N.flow)]
        inputs += [get(N.conv).astype(jnp.float32), get(N.grad_ssm), get(N.bc), rate()]
        inputs += [get(N.small)[2], get(N.enter), leave]
        return reverse_main(*inputs, block, n, into)

    for n in range(seqs):
        add(f"back{n}", lambda n=n: back(n))

    def back_all(n):
        result = get(f"back{seqs - 1}")[n]
        return result.reshape(seqs, rows, channels) if n < 2 else result

    add(N.grad_pre, lambda: tied(N.grad_pre, back_all(0)) * jax.nn.sigmoid(get(N.pre)))
    add(N.grad_pre_low, lambda: get(N.grad_pre).astype(low).reshape(count, channels))

    def proj_part():
        grad_rank = dot(get(N.grad_pre_low), get(N.small)[1], ((1,), (1,)))
        grad_bc = jnp.sum(back_all(2), axis=-1).reshape(count, 2 * NSTATE)
        return jnp.concatenate([grad_rank, grad_bc], axis=1)

    add(N.gpart, proj_part)
    plan.swap(N.yg, lambda: get(N.gpart))
    add(N.grad_proj, lambda: (get(N.gpart) + get(N.yg)).astype(low))

    def grad_mixed():
        product = dot(tied(N.grad_mixed, get(N.grad_proj)), get(N.small)[0], ((1,), (0,)))
        grad_conv = back_all(1) + get(N.small)[8][None] * get(N.grad_ssm)
        grad_conv = grad_conv + product.reshape(seqs, rows, channels)
        return grad_conv * silu_slope(get(N.mixed))

    add(N.grad_mixed, grad_mixed)

    def grad_ext():
        grads = tied(N.grad_ext, get(N.grad_mixed))
        result = jnp.zeros((seqs, rows + reach, channels), jnp.float32)
        for k in range(taps):
            term = get(N.small)[4][k][None, None] * grads * tap_masks[k]
            result = result + jnp.pad(term, ((0, 0), (k, reach - k), (0, 0)))
        return result

    add(N.grad_ext, grad_ext)
    add(N.returned, lambda: shifted(get(N.grad_ext)[:, :reach], DP, -1))

    def grad_inner():
        returned = jnp.pad(get(N.returned), ((0, 0), (rows - reach, 0), (0, 0)))
        result = get(N.grad_ext)[:, reach:] + returned
        return result.astype(low).reshape(count, channels)

    add(N.grad_inner, grad_inner)
    scatter(N.A, lambda: get(N.normed)[0][:count], lambda: tied(N.outA, get(N.grad_inner)), GROUPS[N.A], GROUPS[N.Az])

    def grad_rows():
        pairs = [(tied(N.down, get(N.grad_inner)), get(N.a)), (get(N.grad_gate), pieces_of(get(N.b)))]
        return down(pairs, low)

    add(N.down, grad_rows)
    plan.swap(N.yn, lambda: get(N.down)[1])
    add(N.grad_normed, lambda: tied(N.grad_normed, get(N.down)[0] + get(N.yn).astype(jnp.float32)))
    column = lax.axis_index(TENSOR) * part
    scale = get(N.normed)[1][:count]
    add(N.weighted, lambda: get(N.grad_normed) * lax.dynamic_slice_in_dim(get(N.small)[5], column, part, 0)[None])
    add(N.row_part, lambda: jnp.sum(get(N.weighted) * tokens_f, axis=1, keepdims=True))
    plan.swap(N.yt, lambda: get(N.row_part))

    def input_grad():
        row_total = get(N.row_part) + get(N.yt)
        grads = scale * get(N.weighted) - tokens_f * (scale * scale * scale) * (row_total / features)
        return (cotangent.reshape(count, part).astype(jnp.float32) + grads).reshape(seqs, rows, part)

    def block_out():
        branch = tied(N.block_out, get(N.branch)[0]) + get(N.yb).astype(jnp.float32)
        return (tokens_f + branch).astype(low).reshape(seqs, rows, part)

    def small_grads():
        own, other = get(N.down)
        grads = natural(own, other.astype(jnp.float32))
        x_rows = get(N.rows)[count : 2 * count].astype(jnp.float32)
        grad_gain = jnp.sum(grads * x_rows * scale, axis=0)
        grads = tied(N.taps, get(N.grad_mixed))
        rest = [
            jnp.sum(grads * get(N.extended)[:, k : k + rows] * tap_masks[k], axis=(0, 1))
            for k in range(taps)
        ]
        rest.append(jnp.sum(grads, axis=(0, 1)))
        rest.append(jnp.sum(tied(N.shift, get(N.grad_pre)), axis=(0, 1)))
        conv = get(N.conv).astype(jnp.float32)
        rest.append(jnp.sum(tied(N.skip, get(N.grad_ssm)) * conv, axis=(0, 1)))
        rest.append(grad_gain)
        grad_alog = jnp.sum(back_all(3), axis=0) * get(N.small)[2]
        rest = jnp.concatenate([grad_alog, jnp.stack(rest)], axis=0)
        rest = jnp.pad(rest, ((0, -rest.shape[0] % 16), (0, 0)))
        grad_x_t = dot(tied(N.grad_x, get(N.grad_proj)), get(N.conv_flat), ((0,), (0,)))
        grad_dt = dot(tied(N.grad_dt, get(N.rank)), get(N.grad_pre_low), ((0,), (0,)))
        return deal(grad_x_t, grad_dt, rest)

    pack_steps(plan, N.k, small_grads)
    input_grad, block_out = input_grad(), block_out()
    packed = get(N.k)
    grad_dt = packed[proj_rows : proj_rows + RANK].reshape(devices, -1, shard)
    grad_dt = grad_dt.transpose(1, 0, 2).reshape(-1, channels)
    rest = packed[proj_rows + RANK :]
    by_channel = rest[NSTATE:]
    gain_part = by_channel[taps + 3]
    grad_gain = gain_part + swapped(gain_part, TENSOR)
    grad_in = jnp.stack([get(N.A), get(N.B)], axis=1)
    return (
        block_out,
        input_grad,
        grad_gain,
        grad_in,
        by_channel[:taps],
        by_channel[taps],
        packed[:proj_rows].T,
        grad_dt,
        by_channel[taps + 1],
        rest[:NSTATE].T,
        by_channel[taps + 2],
        get(N.C).T,
    )


def solution(mesh):
    both = (TENSOR, DP)
    devices, halves = mesh.shape[DP], mesh.shape[TENSOR]

    def run(tokens, segments, cotangent, norm_gain, w_in, *others):
        trees = devices == 16 and halves == 2 and w_in.shape[0] == devices * LANES
        trees = trees and w_in.shape[2] == halves * devices * LANES
        return sharded(local if trees else local_whole)(
            tokens, segments, cotangent, norm_gain, w_in, *others
        )

    def sharded(function):
        return jax.shard_map(
            function,
            mesh=mesh,
            in_specs=(
                P(None, DP, TENSOR),
                P(None, DP),
                P(None, DP, TENSOR),
                P(DP),
                P(DP, None, TENSOR),
                P(None, both),
                P(both),
                P(both, None),
                P(DP, TENSOR),
                P(both),
                P(both, None),
                P(both),
                P(TENSOR, DP),
            ),
            out_specs=(
                P(None, DP, TENSOR),
                P(None, DP, TENSOR),
                P(DP),
                P(DP, None, TENSOR),
                P(None, both),
                P(both),
                P(both, None),
                P(DP, TENSOR),
                P(both),
                P(both, None),
                P(both),
                P(TENSOR, DP),
            ),
            check_vma=False,
        )

    return run
```

```python
import functools

import jax
import jax.numpy as jnp
from jax import lax
from jax.experimental import pallas as pl
from jax.experimental.pallas import tpu as pltpu
from jax.sharding import PartitionSpec as P

NSTATE = 16
RANK = 128
LANES = 128
DP = "dp"
TENSOR = "tensor"
GROUP = 8
LOG2E = 1.4426950408889634


def fold(parts, masks):
    width = 1
    while len(parts) > 1:
        joined = []
        for first, second in zip(parts[0::2], parts[1::2]):
            mask = masks[width]
            joined.append(
                jnp.where(mask, first, second) + pltpu.roll(jnp.where(mask, second, first), width, 0)
            )
        parts = joined
        width *= 2
    return parts[0]


def fold_masks():
    row = lax.broadcasted_iota(jnp.int32, (GROUP, LANES), 0)
    return {width: (row & width) == 0 for width in (1, 2, 4)}


def halves(value):
    return value[:GROUP] + value[GROUP:]


def spread(row):
    return jnp.broadcast_to(row, (NSTATE, LANES))


def cols(k):
    return pl.ds(k * LANES, LANES)


def forward_end_kernel(step_ref, flow_ref, b_ref, rate_ref, end_ref):
    groups, unused, width = step_ref.shape
    tiles = width // LANES
    rates = [rate_ref[:, cols(k)] for k in range(tiles)]

    def body(group, states):
        states = list(states)
        for j in range(GROUP):
            t = group * GROUP + j
            b_now = b_ref[t, :NSTATE, :]
            for k in range(tiles):
                decay = jnp.exp2(rates[k] * spread(step_ref[group, j : j + 1, cols(k)]))
                states[k] = decay * states[k] + b_now * spread(flow_ref[group, j : j + 1, cols(k)])
        return tuple(states)

    start = tuple(jnp.zeros((NSTATE, LANES), jnp.float32) for _ in range(tiles))
    ends = lax.fori_loop(0, groups, body, start)
    for k in range(tiles):
        end_ref[:, cols(k)] = ends[k]


def reverse_end_kernel(step_ref, grad_ref, c_ref, rate_ref, end_ref):
    groups, unused, width = step_ref.shape
    tiles = width // LANES
    rates = [rate_ref[:, cols(k)] for k in range(tiles)]

    def body(lap, states):
        states = list(states)
        group = groups - 1 - lap
        for j in reversed(range(GROUP)):
            t = group * GROUP + j
            c_now = c_ref[t, NSTATE:, :]
            for k in range(tiles):
                decay = jnp.exp2(rates[k] * spread(step_ref[group, j : j + 1, cols(k)]))
                states[k] = decay * (states[k] + c_now * spread(grad_ref[group, j : j + 1, cols(k)]))
        return tuple(states)

    start = tuple(jnp.zeros((NSTATE, LANES), jnp.float32) for _ in range(tiles))
    ends = lax.fori_loop(0, groups, body, start)
    for k in range(tiles):
        end_ref[:, cols(k)] = ends[k]


def forward_kernel(step_ref, flow_ref, bc_ref, rate_ref, enter_ref, out_ref):
    groups, unused, width = step_ref.shape
    tiles = width // LANES
    rates = [rate_ref[:, cols(k)] for k in range(tiles)]
    masks = fold_masks()

    def body(group, states):
        states = list(states)
        parts = [[] for _ in range(tiles)]
        for j in range(GROUP):
            t = group * GROUP + j
            b_now, c_now = bc_ref[t, :NSTATE, :], bc_ref[t, NSTATE:, :]
            for k in range(tiles):
                decay = jnp.exp2(rates[k] * spread(step_ref[group, j : j + 1, cols(k)]))
                states[k] = decay * states[k] + b_now * spread(flow_ref[group, j : j + 1, cols(k)])
                parts[k].append(halves(states[k] * c_now))
        for k in range(tiles):
            out_ref[group, :, cols(k)] = fold(parts[k], masks)
        return tuple(states)

    start = tuple(enter_ref[:, cols(k)] for k in range(tiles))
    lax.fori_loop(0, groups, body, start)


def reverse_kernel(
    held,
    step_ref,
    delta_ref,
    flow_ref,
    conv_ref,
    grad_ref,
    bc_ref,
    rate_ref,
    a_ref,
    enter_ref,
    leave_ref,
    *refs,
):
    gdelta_ref, gconv_ref, gbc_ref, ga_ref, decay_scr, state_scr = refs[held:]
    groups, unused, width = step_ref.shape
    tiles = width // LANES
    rates = [rate_ref[:, cols(k)] for k in range(tiles)]
    masks = fold_masks()

    def ahead(group, states):
        states = list(states)
        for j in range(GROUP):
            t = group * GROUP + j
            b_now = bc_ref[t, :NSTATE, :]
            for k in range(tiles):
                decay = jnp.exp2(rates[k] * spread(step_ref[group, j : j + 1, cols(k)]))
                state_scr[t, :, cols(k)] = states[k]
                decay_scr[t, :, cols(k)] = decay
                states[k] = decay * states[k] + b_now * spread(flow_ref[group, j : j + 1, cols(k)])
        return tuple(states)

    start = tuple(enter_ref[:, cols(k)] for k in range(tiles))
    ends = lax.fori_loop(0, groups, ahead, start)
    for k in range(tiles):
        state_scr[groups * GROUP, :, cols(k)] = ends[k]

    @pl.when(pl.program_id(0) == 0)
    def clear():
        gbc_ref[...] = jnp.zeros_like(gbc_ref)

    def back(lap, carried):
        carried, totals = list(carried[0]), list(carried[1])
        group = groups - 1 - lap
        inputs = [[] for _ in range(tiles)]
        drifts = [[] for _ in range(tiles)]
        for j in reversed(range(GROUP)):
            t = group * GROUP + j
            b_now, c_now = bc_ref[t, :NSTATE, :], bc_ref[t, NSTATE:, :]
            sum_b = sum_c = None
            for k in range(tiles):
                grad = spread(grad_ref[group, j : j + 1, cols(k)])
                flow = spread(flow_ref[group, j : j + 1, cols(k)])
                step = spread(delta_ref[group, j : j + 1, cols(k)])
                state_grad = carried[k] + grad * c_now
                inputs[k].insert(0, halves(state_grad * b_now))
                term_b = state_grad * flow
                term_c = state_scr[t + 1, :, cols(k)] * grad
                sum_b = term_b if sum_b is None else sum_b + term_b
                sum_c = term_c if sum_c is None else sum_c + term_c
                carried[k] = decay_scr[t, :, cols(k)] * state_grad
                term = carried[k] * state_scr[t, :, cols(k)]
                drifts[k].insert(0, halves(term * a_ref[:, cols(k)]))
                totals[k] = totals[k] + term * step
            gbc_ref[t, :NSTATE, :] = gbc_ref[t, :NSTATE, :] + sum_b
            gbc_ref[t, NSTATE:, :] = gbc_ref[t, NSTATE:, :] + sum_c
        for k in range(tiles):
            entry = fold(inputs[k], masks)
            gdelta_ref[group, :, cols(k)] = fold(drifts[k], masks) + entry * conv_ref[group, :, cols(k)]
            gconv_ref[group, :, cols(k)] = entry * delta_ref[group, :, cols(k)]
        return (tuple(carried), tuple(totals))

    start = tuple(leave_ref[:, cols(k)] for k in range(tiles))
    zeros = tuple(jnp.zeros((NSTATE, LANES), jnp.float32) for _ in range(tiles))
    unused, totals = lax.fori_loop(0, groups, back, (start, zeros))
    for k in range(tiles):
        ga_ref[:, cols(k)] = totals[k]


def row_spec(rows, width):
    return pl.BlockSpec((None, rows // GROUP, GROUP, width), lambda s, c: (s, 0, 0, c))


def grouped(*arrays):
    return tuple(a.reshape(a.shape[0], -1, GROUP, a.shape[-1]) for a in arrays)


def bc_spec(rows):
    return pl.BlockSpec((None, rows, 2 * NSTATE, LANES), lambda s, c: (s, 0, 0, 0))


def rate_spec(width):
    return pl.BlockSpec((NSTATE, width), lambda s, c: (0, c))


def state_spec(width):
    return pl.BlockSpec((None, NSTATE, width), lambda s, c: (s, 0, c))


def f32(*shape):
    return jax.ShapeDtypeStruct(shape, jnp.float32)


def limits(mb):
    return pltpu.CompilerParams(vmem_limit_bytes=mb * 2**20)


def forward_end(step, flow, bc, rate, width):
    seqs, rows, channels = step.shape
    return pl.pallas_call(
        forward_end_kernel,
        grid=(seqs, channels // width),
        in_specs=[row_spec(rows, width)] * 2 + [bc_spec(rows), rate_spec(width)],
        out_specs=state_spec(width),
        out_shape=f32(seqs, NSTATE, channels),
        compiler_params=limits(40),
        name="forward_end",
    )(*grouped(step, flow), bc, rate)


def reverse_end(step, grad, bc, rate, width):
    seqs, rows, channels = step.shape
    return pl.pallas_call(
        reverse_end_kernel,
        grid=(seqs, channels // width),
        in_specs=[row_spec(rows, width)] * 2 + [bc_spec(rows), rate_spec(width)],
        out_specs=state_spec(width),
        out_shape=f32(seqs, NSTATE, channels),
        compiler_params=limits(40),
        name="reverse_end",
    )(*grouped(step, grad), bc, rate)


def forward_main(step, flow, bc, rate, enter, width):
    seqs, rows, channels = step.shape
    return pl.pallas_call(
        forward_kernel,
        grid=(seqs, channels // width),
        in_specs=[row_spec(rows, width)] * 2 + [bc_spec(rows), rate_spec(width), state_spec(width)],
        out_specs=row_spec(rows, width),
        out_shape=f32(seqs, rows // GROUP, GROUP, channels),
        compiler_params=limits(40),
        name="forward_main",
    )(*grouped(step, flow), bc, rate, enter).reshape(step.shape)


def reverse_main(step, delta, flow, conv, grad, bc, rate, a_mat, enter, leave, width, seq, into=()):
    seqs, rows, channels = step.shape

    def of_seq(*block):
        return pl.BlockSpec((None,) + block, lambda c: (seq,) + (0,) * (len(block) - 1) + (c,))

    row = of_seq(rows // GROUP, GROUP, width)
    state = of_seq(NSTATE, width)
    pairs = pl.BlockSpec((None, rows, 2 * NSTATE, LANES), lambda c: (seq, 0, 0, 0))
    rates = pl.BlockSpec((NSTATE, width), lambda c: (0, c))
    return pl.pallas_call(
        functools.partial(reverse_kernel, len(into)),
        grid=(channels // width,),
        in_specs=[row] * 5
        + [pairs, rates, rates, state, state]
        + [pl.BlockSpec(memory_space=pl.ANY)] * len(into),
        out_specs=[row, row, pairs, state],
        out_shape=[f32(seqs, rows // GROUP, GROUP, channels)] * 2
        + [f32(seqs, rows, 2 * NSTATE, LANES), f32(seqs, NSTATE, channels)],
        input_output_aliases={10 + n: n for n in range(len(into))},
        scratch_shapes=[
            pltpu.VMEM((rows, NSTATE, width), jnp.float32),
            pltpu.VMEM((rows + 1, NSTATE, width), jnp.float32),
        ],
        compiler_params=limits(56),
        name="reverse_main",
    )(*grouped(step, delta, flow, conv, grad), bc, rate, a_mat, enter, leave, *into)


def place_of(piece):
    width = LANES
    return pl.ds(pl.multiple_of((lax.axis_index(DP) ^ piece) * width, width), width)


def piece_spec(n, width, piece=0):
    if n is None:
        return pl.BlockSpec((LANES, width), lambda j: (lax.axis_index(DP) ^ piece, j))
    return pl.BlockSpec((LANES, width), lambda j: (n, j))


def up_kernel(x_ref, *refs):
    pieces, out_ref, x_scr = refs[:-2], refs[-2], refs[-1]

    @pl.when(pl.program_id(0) == 0)
    def order():
        for p in range(len(pieces)):
            x_scr[:, cols(p)] = x_ref[:, place_of(p)]

    weights = jnp.concatenate([ref[...] for ref in pieces], axis=0)
    out_ref[...] = jnp.dot(x_scr[...], weights, preferred_element_type=jnp.float32).astype(
        out_ref.dtype
    )


def up(x, pieces, kind, width=512):
    rows, features = x.shape
    channels = pieces[0][0].shape[1]
    return pl.pallas_call(
        up_kernel,
        grid=(channels // width,),
        in_specs=[pl.BlockSpec((rows, features), lambda j: (0, 0))]
        + [piece_spec(n, width) for unused, n in pieces],
        out_specs=pl.BlockSpec((rows, width), lambda j: (0, j)),
        out_shape=jax.ShapeDtypeStruct((rows, channels), kind),
        scratch_shapes=[pltpu.VMEM((rows, features), x.dtype)],
        compiler_params=limits(40),
        name="up",
    )(x, *[array for array, unused in pieces])


def down_kernel(groups, *refs):
    inputs, pieces = refs[:groups], refs[groups:-3]
    own_ref, other_ref, total = refs[-3:]
    count = len(pieces) // groups
    new = None
    for g, y_ref in enumerate(inputs):
        weights = jnp.concatenate([ref[...] for ref in pieces[g * count : (g + 1) * count]], axis=0)
        term = lax.dot_general(
            y_ref[...], weights, (((1,), (1,)), ((), ())), preferred_element_type=jnp.float32
        )
        new = term if new is None else new + term

    @pl.when(pl.program_id(0) == 0)
    def first():
        total[...] = new

    @pl.when(pl.program_id(0) > 0)
    def later():
        total[...] += new

    @pl.when(pl.program_id(0) == pl.num_programs(0) - 1)
    def last():
        half = count // 2
        mine = lax.axis_index(TENSOR) * half
        for r in range(half):
            own_ref[:, cols(r)] = total[:, place_of(mine + r)]
            other_ref[:, cols(r)] = total[:, place_of((half - mine) + r)].astype(other_ref.dtype)


def down(pairs, kind, width=512):
    rows, channels = pairs[0][0].shape
    count = len(pairs[0][1])
    features = count * LANES
    half = pl.BlockSpec((rows, features // 2), lambda j: (0, 0))
    return pl.pallas_call(
        functools.partial(down_kernel, len(pairs)),
        grid=(channels // width,),
        in_specs=[pl.BlockSpec((rows, width), lambda j: (0, j))] * len(pairs)
        + [
            piece_spec(n, width, piece)
            for unused, pieces in pairs
            for piece, (array, n) in enumerate(pieces)
        ],
        out_specs=[half, half],
        out_shape=[
            jax.ShapeDtypeStruct((rows, features // 2), jnp.float32),
            jax.ShapeDtypeStruct((rows, features // 2), kind),
        ],
        scratch_shapes=[pltpu.VMEM((rows, features), jnp.float32)],
        compiler_params=limits(48),
        name="down",
    )(*[y for y, unused in pairs], *[array for unused, pieces in pairs for array, n in pieces])


def outer_kernel(x_ref, y_ref, *refs):
    outs, x_scr = refs[:-1], refs[-1]

    @pl.when(pl.program_id(0) == 0)
    def order():
        for p in range(x_ref.shape[1] // LANES):
            part = x_ref[:, place_of(p)].astype(jnp.float32)
            x_scr[pl.ds(p * LANES, LANES), :] = part.T.astype(x_scr.dtype)

    product = jnp.dot(x_scr[...], y_ref[...], preferred_element_type=jnp.float32)
    for p in range(product.shape[0] // LANES):
        row = (0, 2, 1, 3)[p // len(outs)] * LANES
        part = product[p * LANES : (p + 1) * LANES]
        outs[p % len(outs)][row : row + LANES, :] = part.astype(outs[0].dtype)


def outer(x, y, width=512):
    rows, features = x.shape
    channels = y.shape[1]
    stacked = features // 4
    return pl.pallas_call(
        outer_kernel,
        grid=(channels // width,),
        in_specs=[
            pl.BlockSpec((rows, features), lambda j: (0, 0)),
            pl.BlockSpec((rows, width), lambda j: (0, j)),
        ],
        out_specs=[pl.BlockSpec((stacked, width), lambda j: (0, j))] * 4,
        out_shape=[jax.ShapeDtypeStruct((stacked, channels), jnp.bfloat16)] * 4,
        scratch_shapes=[pltpu.VMEM((features, rows), x.dtype)],
        compiler_params=limits(48),
        name="outer",
    )(x, y)


def assemble_kernel(blocks, extra_ref, proj_ref, rest_ref, dt_ref):
    depth = dt_ref.shape[0] // (dt_ref.shape[1] // LANES)
    proj_blocks = proj_ref.shape[0] // NSTATE
    odd = lax.rem(lax.axis_index(DP), 2) == 1
    for p in range(0, 16, 2):
        slot = (p >> 2) + (p & 2) * 2
        for core in range(2):
            here = place_of(p + core)
            for b in range(blocks):
                block = extra_ref[core, slot, :NSTATE, cols(b)]
                row = (b if b < proj_blocks else b - proj_blocks) * NSTATE
                if b < proj_blocks:
                    proj_ref[row : row + NSTATE, here] = block
                else:
                    rest_ref[row : row + NSTATE, here] = block.astype(jnp.float32)
        own = extra_ref[0, slot, NSTATE:, :].astype(jnp.float32)[:depth]
        other = extra_ref[1, slot, NSTATE:, :].astype(jnp.float32)[:depth]
        pair = jnp.concatenate(
            [jnp.where(odd, other, own), jnp.where(odd, own, other)], axis=0
        ).astype(dt_ref.dtype)
        first = (lax.axis_index(DP) ^ p) // 2
        dt_ref[pl.ds(pl.multiple_of(first * 2 * depth, 2 * depth), 2 * depth), :] = pair


def assemble(extra, proj_rows, rest_rows):
    channels = extra.shape[-1]
    return pl.pallas_call(
        functools.partial(assemble_kernel, (proj_rows + rest_rows) // NSTATE),
        out_shape=[
            jax.ShapeDtypeStruct((proj_rows, channels), extra.dtype),
            f32(rest_rows, channels),
            jax.ShapeDtypeStruct((RANK, channels), extra.dtype),
        ],
        compiler_params=limits(40),
        name="assemble",
    )(extra)


def deal_kernel(proj_ref, dt_ref, rest_ref, out_ref):
    count = out_ref.shape[0]
    bits = count.bit_length() - 1
    depth = dt_ref.shape[0] // count
    proj_rows = proj_ref.shape[0]
    rest_row = proj_rows + dt_ref.shape[0]
    for n in range(count):
        piece = sum(1 << (bits - 1 - b) for b in range(bits) if n >> b & 1)
        out_ref[n, :proj_rows, :] = proj_ref[:, place_of(piece)].astype(out_ref.dtype)
        out_ref[n, rest_row:, :] = rest_ref[:, place_of(piece)].astype(out_ref.dtype)
        place = pl.ds(pl.multiple_of((lax.axis_index(DP) ^ piece) * depth, depth), depth)
        for k in range(0, count, 2):
            both = jnp.concatenate([dt_ref[place, cols(k)], dt_ref[place, cols(k + 1)]], axis=0)
            row = proj_rows + k * depth
            out_ref[n, row : row + 2 * depth, :] = both.astype(out_ref.dtype)


def deal(proj, dt, rest):
    rows = proj.shape[0] + dt.shape[0] + rest.shape[0]
    return pl.pallas_call(
        deal_kernel,
        out_shape=jax.ShapeDtypeStruct((proj.shape[1] // LANES, rows, LANES), jnp.bfloat16),
        compiler_params=limits(40),
        name="deal",
    )(proj, dt, rest)


EPSILON = 1e-05
RESET = 1e30


def shifted(block, axis, distance):
    devices = range(lax.axis_size(axis))
    route = [(i - distance, i) for i in devices if i - distance in devices]
    return lax.ppermute(block, axis, route)


def swapped(block, axis):
    return lax.ppermute(block, axis, [(0, 1), (1, 0)])


def exchanged(block, mask):
    return lax.ppermute(block, DP, [(i, i ^ mask) for i in range(lax.axis_size(DP))])


def after(block, *earlier):
    return lax.optimization_barrier((block, *earlier))[0] if earlier else block


def sent(block, mask, name, *earlier):
    with jax.named_scope(f"{name}_to_{mask}"):
        return exchanged(after(block, *earlier), mask)


def round_masks():
    return [1 << n for n in range(lax.axis_size(DP).bit_length() - 1)]


def total(*blocks):
    result = blocks[0].astype(jnp.float32)
    for block in blocks[1:]:
        result = result + block.astype(jnp.float32)
    return result


def silu_slope(values):
    squash = jax.nn.sigmoid(values)
    return squash * (1.0 + values * (1.0 - squash))


def dot(left, right, dims):
    return lax.dot_general(left, right, (dims, ((), ())), preferred_element_type=jnp.float32)


def joined(block, axis):
    if lax.axis_size(axis) != 2:
        return lax.all_gather(block, axis, axis=block.ndim - 1, tiled=True)
    other = swapped(block, axis)
    first = lax.axis_index(axis) == 0
    return jnp.concatenate(
        [jnp.where(first, block, other), jnp.where(first, other, block)], axis=-1
    )


def summed(block, axis):
    if lax.axis_size(axis) != 2:
        return lax.psum(block, axis)
    return block + swapped(block, axis)


def sum_scattered(block, axis):
    last = block.ndim - 1
    if lax.axis_size(axis) != 2:
        return lax.psum_scatter(block, axis, scatter_dimension=last, tiled=True)
    width = block.shape[-1] // 2
    place = lax.axis_index(axis)
    own = lax.dynamic_slice_in_dim(block, place * width, width, last)
    other = lax.dynamic_slice_in_dim(block, (1 - place) * width, width, last)
    return own + swapped(other, axis)


def entering(value, span, rate, axis, direction):
    value = shifted(value, axis, direction)
    span = shifted(span, axis, direction)
    distance = 1
    while distance < lax.axis_size(axis):
        further = shifted(value, axis, direction * distance)
        further_span = shifted(span, axis, direction * distance)
        value = value + jnp.exp2(rate[None] * span[:, None, :]) * further
        span = span + further_span
        distance *= 2
    return value


def local_whole(
    tokens, segments, cotangent, norm_gain, w_in, conv_w, conv_b, w_x, w_dt, dt_bias, a_log, d_skip, w_out
):
    seqs, rows, part = tokens.shape
    features, channels = part * lax.axis_size(TENSOR), w_in.shape[2]
    devices = lax.axis_size(DP)
    shard = channels // devices
    taps = conv_w.shape[0]
    reach = taps - 1
    block = min(512, channels)
    count = seqs * rows
    low = jnp.bfloat16

    small = jnp.concatenate(
        [
            conv_w,
            conv_b[None],
            dt_bias[None],
            d_skip[None],
            a_log.T,
            w_x.T,
            w_dt.reshape(-1, shard),
            norm_gain.reshape(-1, shard),
        ],
        axis=0,
    )
    small = lax.all_gather(small, DP)
    w_in_x = lax.all_gather(w_in[:, 0], DP, axis=0, tiled=True)
    w_in_gate = lax.all_gather(w_in[:, 1], DP, axis=0, tiled=True)
    w_out_t = lax.all_gather(w_out.T, DP, axis=0, tiled=True)
    channel_rows = taps + 3 + NSTATE + w_x.shape[1]
    by_channel = small[:, :channel_rows].transpose(1, 0, 2).reshape(channel_rows, channels)
    taps_f = by_channel[:taps].astype(jnp.float32)
    bias_f, shift_f, skip_f = (by_channel[taps + i].astype(jnp.float32)[None] for i in range(3))
    a_mat = -jnp.exp(by_channel[taps + 3 : taps + 3 + NSTATE].astype(jnp.float32))
    rate = a_mat * LOG2E
    w_x_t = by_channel[taps + 3 + NSTATE :]
    dt_full = small[:, channel_rows : channel_rows + RANK].reshape(RANK, channels)
    gain_f = small[:, channel_rows + RANK :].reshape(features).astype(jnp.float32)

    marks_own = segments + 1
    marks_before = shifted(marks_own[:, rows - reach :], DP, 1)
    marks = jnp.concatenate([marks_before, marks_own], axis=1)
    tail = shifted(tokens[:, rows - reach :], DP, 1)
    wanted = jnp.concatenate(
        [tokens.reshape(count, part), tail.reshape(seqs * reach, part)], axis=0
    )
    x_rows = joined(wanted, TENSOR).astype(jnp.float32)
    cot = joined(cotangent.reshape(count, part), TENSOR)
    scale_all = lax.rsqrt(jnp.mean(x_rows * x_rows, axis=1, keepdims=True) + EPSILON)
    normed_all = (x_rows * scale_all * gain_f[None]).astype(low)
    normed, scale = normed_all[:count], scale_all[:count]

    inner_all = dot(normed_all, w_in_x, ((1,), (0,))).astype(low)
    inner_ext = jnp.concatenate(
        [
            inner_all[count:].reshape(seqs, reach, channels),
            inner_all[:count].reshape(seqs, rows, channels),
        ],
        axis=1,
    ).astype(jnp.float32)
    tap_masks = [
        (marks[:, k : k + rows] == marks_own).astype(jnp.float32)[:, :, None] for k in range(taps)
    ]
    mixed = bias_f[None]
    for k in range(taps):
        mixed = mixed + taps_f[k][None, None] * inner_ext[:, k : k + rows] * tap_masks[k]
    conv_low = jax.nn.silu(mixed).astype(low)
    conv = conv_low.astype(jnp.float32)
    conv_flat = conv_low.reshape(count, channels)
    proj = summed(dot(conv_flat, w_x_t, ((1,), (1,))), TENSOR)
    rank_part = proj[:, :RANK].astype(low)
    bc = jnp.broadcast_to(
        proj[:, RANK:].reshape(seqs, rows, 2 * NSTATE, 1), (seqs, rows, 2 * NSTATE, LANES)
    )
    pre = (dot(rank_part, dt_full, ((1,), (0,))) + shift_f).reshape(seqs, rows, channels)
    delta = jax.nn.softplus(pre)
    step = jnp.where(tap_masks[reach - 1] > 0, delta, RESET)
    flow = delta * conv
    span = jnp.sum(step, axis=1)

    end = forward_end(step, flow, bc, rate, block)
    enter = entering(end, span, rate, DP, 1)
    readout = forward_main(step, flow, bc, rate, enter, block)
    ssm = readout + skip_f[None] * conv

    gate = dot(normed, w_in_gate, ((1,), (0,))).reshape(seqs, rows, channels)
    silu_gate = jax.nn.silu(gate)
    gated = (ssm * silu_gate).astype(low).reshape(count, channels)
    branch = sum_scattered(dot(gated, w_out_t, ((1,), (1,))), TENSOR)
    tokens_f = tokens.reshape(count, part).astype(jnp.float32)
    block_out = (tokens_f + branch).astype(low).reshape(seqs, rows, part)
    grad_out_t = dot(cot, gated, ((0,), (0,))).astype(low)
    grad_out_t = lax.psum_scatter(grad_out_t, DP, scatter_dimension=0, tiled=True)
    grad_gated = dot(cot, w_out_t, ((1,), (0,))).reshape(seqs, rows, channels)
    grad_ssm = grad_gated * silu_gate
    grad_gate = (grad_gated * ssm * silu_slope(gate)).astype(low).reshape(count, channels)
    grad_in_gate = dot(normed, grad_gate, ((0,), (0,))).astype(low)
    grad_in_gate = lax.psum_scatter(grad_in_gate, DP, scatter_dimension=0, tiled=True)
    grad_skip = jnp.sum(grad_ssm * conv, axis=(0, 1))

    back_end = reverse_end(step, grad_ssm, bc, rate, block)
    leave = entering(back_end, span, rate, DP, -1)
    back = ()
    for n in range(seqs):
        back = reverse_main(
            step, delta, flow, conv, grad_ssm, bc, rate, a_mat, enter, leave, block, n, back
        )
    grad_delta, grad_conv_scan, grad_bc, grad_a = back
    grad_delta, grad_conv_scan = (part.reshape(step.shape) for part in (grad_delta, grad_conv_scan))
    grad_alog = jnp.sum(grad_a, axis=0) * a_mat
    grad_pre = grad_delta * jax.nn.sigmoid(pre)
    grad_shift = jnp.sum(grad_pre, axis=(0, 1))
    grad_pre_low = grad_pre.astype(low).reshape(count, channels)
    grad_dt = dot(rank_part, grad_pre_low, ((0,), (0,)))
    grad_rank = dot(grad_pre_low, dt_full, ((1,), (1,)))
    grad_proj = jnp.concatenate(
        [grad_rank, jnp.sum(grad_bc, axis=-1).reshape(count, 2 * NSTATE)], axis=1
    )
    grad_proj = summed(grad_proj, TENSOR).astype(low)
    grad_x_t = dot(grad_proj, conv_flat, ((0,), (0,)))
    grad_conv = (
        grad_conv_scan
        + skip_f[None] * grad_ssm
        + dot(grad_proj, w_x_t, ((1,), (0,))).reshape(seqs, rows, channels)
    )
    grad_mixed = grad_conv * silu_slope(mixed)
    grad_bias = jnp.sum(grad_mixed, axis=(0, 1))
    grad_taps = jnp.stack(
        [
            jnp.sum(grad_mixed * inner_ext[:, k : k + rows] * tap_masks[k], axis=(0, 1))
            for k in range(taps)
        ]
    )
    grad_ext = jnp.zeros((seqs, rows + reach, channels), jnp.float32)
    for k in range(taps):
        grad_ext = grad_ext + jnp.pad(
            taps_f[k][None, None] * grad_mixed * tap_masks[k], ((0, 0), (k, reach - k), (0, 0))
        )
    returned = shifted(grad_ext[:, :reach], DP, -1)
    grad_inner = grad_ext[:, reach:] + jnp.pad(returned, ((0, 0), (rows - reach, 0), (0, 0)))
    grad_inner = grad_inner.astype(low).reshape(count, channels)
    grad_in_x = dot(normed, grad_inner, ((0,), (0,))).astype(low)
    grad_in_x = lax.psum_scatter(grad_in_x, DP, scatter_dimension=0, tiled=True)

    grad_normed = sum_scattered(
        dot(grad_inner, w_in_x, ((1,), (1,))) + dot(grad_gate, w_in_gate, ((1,), (1,))), TENSOR
    )
    column = lax.axis_index(TENSOR) * part
    gain_local = lax.dynamic_slice_in_dim(gain_f, column, part, 0)
    weighted = grad_normed * gain_local[None]
    grad_gain = jnp.sum(grad_normed * tokens_f * scale, axis=0)
    grad_gain = lax.dynamic_update_slice_in_dim(
        jnp.zeros((features,), jnp.float32), grad_gain, column, 0
    )
    row_total = summed(jnp.sum(weighted * tokens_f, axis=1, keepdims=True), TENSOR)
    input_grad = (
        cotangent.reshape(count, part).astype(jnp.float32)
        + scale * weighted
        - tokens_f * (scale * scale * scale) * (row_total / features)
    ).reshape(seqs, rows, part)

    by_channel = jnp.concatenate(
        [grad_taps, grad_bias[None], grad_shift[None], grad_skip[None], grad_alog, grad_x_t], axis=0
    )
    by_channel = by_channel.reshape(channel_rows, devices, shard).transpose(1, 0, 2)
    packed = jnp.concatenate(
        [
            by_channel,
            grad_dt.reshape(devices, RANK, shard),
            grad_gain.reshape(devices, -1, shard),
        ],
        axis=1,
    )
    packed = lax.psum_scatter(packed, DP, scatter_dimension=0)
    by_channel = packed[:channel_rows]
    grad_dt = packed[channel_rows : channel_rows + RANK].reshape(-1, channels)
    grad_gain = summed(packed[channel_rows + RANK :], TENSOR).reshape(-1)
    grad_in = jnp.stack([grad_in_x, grad_in_gate], axis=1).astype(jnp.float32)
    return (
        block_out,
        input_grad,
        grad_gain,
        grad_in,
        by_channel[:taps],
        by_channel[taps],
        by_channel[taps + 3 + NSTATE :].T,
        grad_dt,
        by_channel[taps + 1],
        by_channel[taps + 3 : taps + 3 + NSTATE].T,
        by_channel[taps + 2],
        grad_out_t.astype(jnp.float32).T,
    )


class Names:
    def __getattr__(self, name):
        return name


N = Names()


class Plan:
    def __init__(self, waits):
        self.waits, self.steps, self.values, self.open = waits, {}, {}, set()

    def add(self, name, step):
        self.steps[name] = step

    def get(self, name):
        if name not in self.values:
            if name in self.open:
                raise ValueError(f"cycle at {name}")
            self.open.add(name)
            self.values[name] = self.steps[name]()
            self.open.remove(name)
        return self.values[name]

    def first(self, name):
        value = self.get(name)
        return value[0] if isinstance(value, (tuple, list)) else value

    def tied(self, name, block):
        return after(block, *(self.first(other) for other in self.waits.get(name, ())))

    def send(self, name, block, mask):
        def step():
            with jax.named_scope(name):
                return exchanged(self.tied(name, block()), mask)

        self.add(name, step)

    def swap(self, name, block):
        def step():
            with jax.named_scope(name):
                return swapped(self.tied(name, block()), TENSOR)

        self.add(name, step)


def gather_steps(plan, chunk, shard, groups, rows):
    places = {}

    def block(pieces):
        parts = []
        for n, piece in enumerate(pieces):
            name, row = places[piece]
            array = plan.get(name) if name else shard()
            part = array[row * LANES : row * LANES + rows] if array.shape[0] != rows else array
            parts.append(part)
        return parts[0] if len(parts) == 1 else jnp.concatenate(parts, axis=0)

    def move(name, pieces, mask):
        def start():
            return block(pieces)

        plan.send(name, start, mask)
        for n, piece in enumerate(pieces):
            places[piece + mask] = (name, n)

    places[0] = (None, 0)
    move(f"{chunk}4", (0,), 4)
    move(f"{chunk}8", (0,), 8)
    move(f"{chunk}12", (8,), 4)
    for group in groups:
        move(f"{chunk}x{group[0]}", group, 2)

    def core(name, pieces):
        first, *others = (block((p,))[:LANES] for p in pieces)
        return jnp.concatenate([plan.tied(name, first), *others], axis=0)

    for x in (0, 2):
        name, pieces = f"{chunk}s{x}", [z + x for z in (0, 4, 8, 12)]
        plan.send(name, lambda name=name, pieces=pieces: core(name, pieces), 1)
        for n, piece in enumerate(pieces):
            places[piece + 1] = (name, n)

    def pieces():
        return [(plan.get(places[p][0]) if places[p][0] else shard(), places[p][1]) for p in range(16)]

    def extra():
        return jnp.stack([block((p,))[LANES:] for p in (0, 4, 8, 12, 2, 6, 10, 14)])

    plan.add(chunk, pieces)
    if rows > LANES:
        plan.add(f"{chunk}own", extra)
        plan.send(f"{chunk}e", lambda: plan.get(f"{chunk}own"), 1)


ROWS = {0: 0, 8: 1, 4: 2, 12: 3}


def scatter_steps(plan, name, outer_name, groups, near_groups):
    crossed, neared = {}, {}

    def rows_of(group):
        first = ROWS[group[0]]
        return slice(first * LANES, (first + len(group)) * LANES)

    def chip(x, group):
        return [plan.get(outer_name)[x][rows_of(group)], plan.get(f"{name}s{x}")[rows_of(group)]]

    def pick(table, z):
        step, n = table[z]
        return plan.get(step)[n * LANES : (n + 1) * LANES]

    for x in (2, 0):
        plan.send(f"{name}s{x}", lambda x=x: plan.get(outer_name)[x + 1], 1)
    for group in groups:
        ready, step = f"{name}p{group[0]}", f"{name}x{group[0]}"
        plan.add(ready, lambda group=group: total(*chip(2, group)).astype(jnp.bfloat16))
        plan.send(step, lambda ready=ready: plan.get(ready), 2)
        for n, z in enumerate(group):
            crossed[z] = (step, n)

    def column(group):
        parts = [
            total(*chip(0, (z,)), pick(crossed, z), *([pick(neared, z)] if z == 8 else [])) for z in group
        ]
        return jnp.concatenate(parts, axis=0).astype(jnp.bfloat16)

    for group in near_groups:
        step = f"{name}z{group[0]}"
        plan.send(step, lambda group=group: column(group), 4)
        for n, z in enumerate(group):
            neared[z - 4] = (step, n)
    plan.send(f"{name}z8", lambda: column((8,)), 8)

    def result():
        last = plan.tied(name, plan.get(f"{name}z8"))
        return total(last, pick(neared, 0), pick(crossed, 0), *chip(0, (0,)))

    plan.add(name, result)


def state_steps(plan, name, value, span, rate, known=None):
    low = jnp.bfloat16

    def message(n):
        mask = round_masks()[n]
        lower = lax.rem(lax.div(lax.axis_index(DP), mask), 2) == 0
        now = plan.get(f"{name}in{n}")
        got = plan.get(f"{name}{n}")
        other = got[:, :NSTATE].astype(jnp.float32)
        own_span, other_span, before, behind = plan.get(f"{known or name}spans{n}")
        first = ~lower if known else lower
        far = jnp.where(first, 0.0, other)
        decay = lambda steps: jnp.exp2(rate()[None] * steps[:, None, :])
        result = far if n == 0 else now[1] + decay(behind if known else before) * far
        through = jnp.where(first, other_span, own_span)
        value = jnp.where(first, other, now[0]) + decay(through) * jnp.where(first, now[0], other)
        return value, result

    def spans(n):
        if n == 0:
            own, before, behind = span(), jnp.zeros_like(span()), jnp.zeros_like(span())
        else:
            own, other, before, behind = plan.get(f"{name}spans{n - 1}")
            lower = lax.rem(lax.div(lax.axis_index(DP), round_masks()[n - 1]), 2) == 0
            before = before + jnp.where(lower, 0.0, other)
            behind = behind + jnp.where(lower, other, 0.0)
            own = own + other
        with jax.named_scope(f"{name}span{n}"):
            other = exchanged(plan.tied(f"{name}span{n}", own), round_masks()[n])
        return own, other, before, behind

    count = len(round_masks())
    for n in range(count):
        plan.add(f"{name}in{n}", lambda n=n: message(n - 1) if n else (value(), None))
        plan.send(f"{name}{n}", lambda n=n: plan.get(f"{name}in{n}")[0].astype(low), round_masks()[n])
        if not known:
            plan.add(f"{name}spans{n}", lambda n=n: spans(n))
    plan.add(name, lambda: message(count - 1)[1])


def pack_steps(plan, name, blocks):
    def sums(n):
        if n == 0:
            return blocks()
        before = sums_of(n - 1)
        half = before.shape[0] // 2
        return before[:half].astype(jnp.float32) + plan.get(f"{name}{n - 1}").astype(jnp.float32)

    def sums_of(n):
        return plan.get(f"{name}sum{n}")

    def sent_half(n):
        block = sums_of(n)
        return block[block.shape[0] // 2 :].astype(jnp.bfloat16)

    for n in range(len(round_masks()) + 1):
        plan.add(f"{name}sum{n}", lambda n=n: sums(n))
    for n, mask in enumerate(round_masks()):
        plan.send(f"{name}{n}", lambda n=n: sent_half(n), mask)
    plan.add(name, lambda: sums_of(len(round_masks()))[0])


WAITS = dict(
    a12=(N.a4, N.a8, N.ax0, N.bx0),
    ax4=(N.a4, N.a8, N.ax0, N.bx0),
    ax8=(N.a4, N.a8, N.ax0, N.bx0),
    b4=(N.a12,),
    b8=(N.a12,),
    ax12=(N.ax4, N.ax8, N.a12),
    as0=(N.ax4, N.ax8, N.a12),
    as2=(N.b4, N.b8),
    bx4=(N.as0, N.as2, N.ae),
    b12=(N.inner,),
    bx12=(N.f1,),
    bs0=(N.f1,),
    gate=(N.readout,),
    outB=(N.r0,),
    branch=(N.outB,),
    back0=(N.branch,),
    taps=(N.grad_normed,),
    c=(N.inner,),
    grad_gated=(N.outC,),
    back1=(N.Bx4,),
    grad_mixed=(N.Bx0, N.Bz12, N.yb),
    Bz8=(N.Ap4,),
    down=(N.Ap4, N.As0),
    Ax0=(N.Ap4,),
    yn=(N.Ax4,),
    y0=(N.ax0,),
    bs2=(N.readout,),
    grad_pre=(N.Bx4,),
    Az12=(N.As0,),
    ae=(N.ax8,),
    grad_normed=(N.Bz8,),
)
GROUPS = dict(
    a=((0,), (4,), (8,), (12,)),
    b=((0,), (4,), (8,), (12,)),
    c=(),
    C=(),
    B=((4, 12), (0, 8)),
    A=((4, 12), (0, 8)),
    Cz=(),
    Bz=((12,), (4,)),
    Az=((12,), (4,)),
)


def local(
    tokens, segments, cotangent, norm_gain, w_in, conv_w, conv_b, w_x, w_dt, dt_bias, a_log, d_skip, w_out
):
    seqs, rows, part = tokens.shape
    features, channels = part * 2, w_in.shape[2]
    devices = lax.axis_size(DP)
    shard = channels // devices
    taps = conv_w.shape[0]
    reach = taps - 1
    block = min(512, channels)
    count = seqs * rows
    low = jnp.bfloat16
    plan = Plan(WAITS)
    get, add, tied = plan.get, plan.add, plan.tied
    first_half = lax.axis_index(TENSOR) == 0

    def natural(own, other):
        return jnp.concatenate(
            [jnp.where(first_half, own, other), jnp.where(first_half, other, own)], axis=-1
        )

    def up_any(x, weights):
        if isinstance(weights, list):
            return up(x, weights, jnp.float32)
        return dot(x, weights, ((1,), (0,)))

    def pieces_of(weights):
        return weights if isinstance(weights, list) else [(weights, None)] * devices

    proj_rows = w_x.shape[1]
    small = jnp.concatenate(
        [
            w_x.T,
            a_log.T,
            conv_w,
            conv_b[None],
            dt_bias[None],
            d_skip[None],
            norm_gain.reshape(-1, shard),
        ],
        axis=0,
    )
    rest_rows = small.shape[0] - proj_rows
    rest_rows += -rest_rows % NSTATE
    small = jnp.pad(small, ((0, channels // LANES * NSTATE - small.shape[0]), (0, 0)))
    small = small.reshape(-1, NSTATE, LANES).transpose(1, 0, 2).reshape(NSTATE, channels)
    steps = jnp.pad(w_dt, ((0, NSTATE - w_dt.shape[0]), (0, 0)))
    shard_x = jnp.concatenate([w_in[:, 0], small, steps], axis=0)
    shard_gate, shard_out = w_in[:, 1], w_out.T
    gather_steps(plan, N.a, lambda: shard_x, GROUPS[N.a], shard_x.shape[0])
    for name, held in ((N.b, shard_gate), (N.c, shard_out)):
        if GROUPS[name]:
            gather_steps(plan, name, lambda held=held: held, GROUPS[name], LANES)
        else:
            add(name, lambda name=name, held=held: lax.all_gather(tied(name, held), DP, axis=0, tiled=True))

    def small_weights():
        extra = jnp.stack([get(N.aown), get(N.ae)])
        w_x_t, rest, dt_full = assemble(tied(N.small, extra), proj_rows, rest_rows)
        a_mat = -jnp.exp(rest[:NSTATE])
        gain = rest[NSTATE + taps + 3]
        others = [rest[NSTATE + taps + i][None] for i in range(3)]
        return w_x_t, dt_full, a_mat, a_mat * LOG2E, rest[NSTATE : NSTATE + taps], gain, *others

    add(N.small, small_weights)

    marks_own = segments + 1
    marks_before = shifted(marks_own[:, rows - reach :], DP, 1)
    marks = jnp.concatenate([marks_before, marks_own], axis=1)
    tap_masks = [
        (marks[:, k : k + rows] == marks_own).astype(jnp.float32)[:, :, None] for k in range(taps)
    ]
    tail = shifted(tokens[:, rows - reach :], DP, 1)
    wanted = [cotangent.reshape(count, part), tokens.reshape(count, part)]
    wanted.append(tail.reshape(seqs * reach, part))
    wanted = jnp.concatenate(wanted, axis=0)
    wanted = jnp.pad(wanted, ((0, -wanted.shape[0] % 16), (0, 0)))
    tokens_f = tokens.reshape(count, part).astype(jnp.float32)
    plan.swap(N.y0, lambda: wanted)
    add(N.rows, lambda: natural(wanted, get(N.y0)))

    def normed():
        x_rows = get(N.rows)[count:].astype(jnp.float32)
        scale = lax.rsqrt(jnp.mean(x_rows * x_rows, axis=1, keepdims=True) + EPSILON)
        return (x_rows * scale * get(N.small)[5][None]).astype(low), scale

    add(N.normed, normed)
    add(N.cot, lambda: get(N.rows)[:count])

    add(N.inner, lambda: up(tied(N.inner, get(N.normed)[0]), get(N.a), low))

    def extended():
        inner = get(N.inner)
        before = inner[count : count + seqs * reach].reshape(seqs, reach, channels)
        now = inner[:count].reshape(seqs, rows, channels)
        return jnp.concatenate([before, now], axis=1).astype(jnp.float32)

    add(N.extended, extended)

    def mixed():
        taps_f, bias_f = get(N.small)[4], get(N.small)[6]
        result = bias_f[None]
        for k in range(taps):
            result = result + taps_f[k][None, None] * get(N.extended)[:, k : k + rows] * tap_masks[k]
        return result

    add(N.mixed, mixed)
    add(N.conv, lambda: jax.nn.silu(get(N.mixed)).astype(low))
    add(N.conv_flat, lambda: get(N.conv).reshape(count, channels))
    add(N.part, lambda: dot(get(N.conv_flat), get(N.small)[0], ((1,), (1,))))
    plan.swap(N.yp, lambda: get(N.part))
    add(N.proj, lambda: get(N.part) + get(N.yp))
    add(N.rank, lambda: get(N.proj)[:, :RANK].astype(low))

    def broadcast():
        columns = get(N.proj)[:, RANK:].reshape(seqs, rows, 2 * NSTATE, 1)
        return jnp.broadcast_to(columns, (seqs, rows, 2 * NSTATE, LANES))

    add(N.bc, broadcast)

    def pre():
        product = dot(get(N.rank), get(N.small)[1], ((1,), (0,)))
        return (product + get(N.small)[7]).reshape(seqs, rows, channels)

    add(N.pre, pre)
    add(N.delta, lambda: jax.nn.softplus(get(N.pre)))
    add(N.step, lambda: jnp.where(tap_masks[reach - 1] > 0, get(N.delta), RESET))
    add(N.flow, lambda: get(N.delta) * get(N.conv).astype(jnp.float32))
    add(N.span, lambda: jnp.sum(get(N.step), axis=1))

    def rate():
        return get(N.small)[3]

    add(N.end, lambda: forward_end(get(N.step), tied(N.end, get(N.flow)), get(N.bc), rate(), block))
    state_steps(plan, N.f, lambda: get(N.end), lambda: get(N.span), rate)
    add(N.enter, lambda: get(N.f))
    add(
        N.readout,
        lambda: forward_main(
            get(N.step), get(N.flow), get(N.bc), rate(), tied(N.readout, get(N.enter)), block
        ),
    )
    add(N.ssm, lambda: get(N.readout) + get(N.small)[8][None] * get(N.conv).astype(jnp.float32))

    def gate():
        own = tied(N.gate, get(N.normed)[0][:count])
        return up_any(own, get(N.b)).reshape(seqs, rows, channels)

    add(N.gate, gate)
    add(N.silu_gate, lambda: jax.nn.silu(get(N.gate)))
    add(N.gated, lambda: (get(N.ssm) * get(N.silu_gate)).astype(low).reshape(count, channels))
    def scatter(name, x, y, groups, near):
        if groups:
            add(f"out{name}", lambda: outer(x(), y()))
            scatter_steps(plan, name, f"out{name}", groups, near)
        else:
            add(f"out{name}", lambda: dot(x(), y(), ((0,), (0,))).astype(low))
            add(
                f"{name}rs",
                lambda: lax.psum_scatter(
                    tied(f"{name}rs", get(f"out{name}")), DP, scatter_dimension=0, tiled=True
                ),
            )
            add(name, lambda: tied(name, get(f"{name}rs")).astype(jnp.float32))

    scatter(N.C, lambda: get(N.cot), lambda: tied(N.outC, get(N.gated)), GROUPS[N.C], GROUPS[N.Cz])
    add(N.grad_gated, lambda: up_any(tied(N.grad_gated, get(N.cot)), get(N.c)))
    add(N.grad_gated3, lambda: get(N.grad_gated).reshape(seqs, rows, channels))
    add(N.grad_ssm, lambda: tied(N.grad_ssm, get(N.grad_gated3)) * get(N.silu_gate))

    def grad_gate():
        slope = silu_slope(get(N.gate))
        result = tied(N.grad_gate, get(N.grad_gated3)) * get(N.ssm) * slope
        return result.astype(low).reshape(count, channels)

    add(N.grad_gate, grad_gate)

    add(
        N.rend,
        lambda: reverse_end(get(N.step), tied(N.rend, get(N.grad_ssm)), get(N.bc), rate(), block),
    )
    state_steps(plan, N.r, lambda: get(N.rend), None, rate, N.f)
    scatter(N.B, lambda: get(N.normed)[0][:count], lambda: tied(N.outB, get(N.grad_gate)), GROUPS[N.B], GROUPS[N.Bz])
    add(N.branch, lambda: down([(tied(N.branch, get(N.gated)), pieces_of(get(N.c)))], low))
    plan.swap(N.yb, lambda: get(N.branch)[1])

    def back(n):
        into = get(f"back{n - 1}") if n else ()
        leave = tied(f"back{n}", get(N.r))
        inputs = [get(N.step), get(N.delta), get(N.flow)]
        inputs += [get(N.conv).astype(jnp.float32), get(N.grad_ssm), get(N.bc), rate()]
        inputs += [get(N.small)[2], get(N.enter), leave]
        return reverse_main(*inputs, block, n, into)

    for n in range(seqs):
        add(f"back{n}", lambda n=n: back(n))

    def back_all(n):
        result = get(f"back{seqs - 1}")[n]
        return result.reshape(seqs, rows, channels) if n < 2 else result

    add(N.grad_pre, lambda: tied(N.grad_pre, back_all(0)) * jax.nn.sigmoid(get(N.pre)))
    add(N.grad_pre_low, lambda: get(N.grad_pre).astype(low).reshape(count, channels))

    def proj_part():
        grad_rank = dot(get(N.grad_pre_low), get(N.small)[1], ((1,), (1,)))
        grad_bc = jnp.sum(back_all(2), axis=-1).reshape(count, 2 * NSTATE)
        return jnp.concatenate([grad_rank, grad_bc], axis=1)

    add(N.gpart, proj_part)
    plan.swap(N.yg, lambda: get(N.gpart))
    add(N.grad_proj, lambda: (get(N.gpart) + get(N.yg)).astype(low))

    def grad_mixed():
        product = dot(tied(N.grad_mixed, get(N.grad_proj)), get(N.small)[0], ((1,), (0,)))
        grad_conv = back_all(1) + get(N.small)[8][None] * get(N.grad_ssm)
        grad_conv = grad_conv + product.reshape(seqs, rows, channels)
        return grad_conv * silu_slope(get(N.mixed))

    add(N.grad_mixed, grad_mixed)

    def grad_ext():
        grads = tied(N.grad_ext, get(N.grad_mixed))
        result = jnp.zeros((seqs, rows + reach, channels), jnp.float32)
        for k in range(taps):
            term = get(N.small)[4][k][None, None] * grads * tap_masks[k]
            result = result + jnp.pad(term, ((0, 0), (k, reach - k), (0, 0)))
        return result

    add(N.grad_ext, grad_ext)
    add(N.returned, lambda: shifted(get(N.grad_ext)[:, :reach], DP, -1))

    def grad_inner():
        returned = jnp.pad(get(N.returned), ((0, 0), (rows - reach, 0), (0, 0)))
        result = get(N.grad_ext)[:, reach:] + returned
        return result.astype(low).reshape(count, channels)

    add(N.grad_inner, grad_inner)
    scatter(N.A, lambda: get(N.normed)[0][:count], lambda: tied(N.outA, get(N.grad_inner)), GROUPS[N.A], GROUPS[N.Az])

    def grad_rows():
        pairs = [(tied(N.down, get(N.grad_inner)), get(N.a)), (get(N.grad_gate), pieces_of(get(N.b)))]
        return down(pairs, low)

    add(N.down, grad_rows)
    plan.swap(N.yn, lambda: get(N.down)[1])
    add(N.grad_normed, lambda: tied(N.grad_normed, get(N.down)[0] + get(N.yn).astype(jnp.float32)))
    column = lax.axis_index(TENSOR) * part
    scale = get(N.normed)[1][:count]
    add(N.weighted, lambda: get(N.grad_normed) * lax.dynamic_slice_in_dim(get(N.small)[5], column, part, 0)[None])
    add(N.row_part, lambda: jnp.sum(get(N.weighted) * tokens_f, axis=1, keepdims=True))
    plan.swap(N.yt, lambda: get(N.row_part))

    def input_grad():
        row_total = get(N.row_part) + get(N.yt)
        grads = scale * get(N.weighted) - tokens_f * (scale * scale * scale) * (row_total / features)
        return (cotangent.reshape(count, part).astype(jnp.float32) + grads).reshape(seqs, rows, part)

    def block_out():
        branch = tied(N.block_out, get(N.branch)[0]) + get(N.yb).astype(jnp.float32)
        return (tokens_f + branch).astype(low).reshape(seqs, rows, part)

    def small_grads():
        own, other = get(N.down)
        grads = natural(own, other.astype(jnp.float32))
        x_rows = get(N.rows)[count : 2 * count].astype(jnp.float32)
        grad_gain = jnp.sum(grads * x_rows * scale, axis=0)
        grads = tied(N.taps, get(N.grad_mixed))
        rest = [
            jnp.sum(grads * get(N.extended)[:, k : k + rows] * tap_masks[k], axis=(0, 1))
            for k in range(taps)
        ]
        rest.append(jnp.sum(grads, axis=(0, 1)))
        rest.append(jnp.sum(tied(N.shift, get(N.grad_pre)), axis=(0, 1)))
        conv = get(N.conv).astype(jnp.float32)
        rest.append(jnp.sum(tied(N.skip, get(N.grad_ssm)) * conv, axis=(0, 1)))
        rest.append(grad_gain)
        grad_alog = jnp.sum(back_all(3), axis=0) * get(N.small)[2]
        rest = jnp.concatenate([grad_alog, jnp.stack(rest)], axis=0)
        rest = jnp.pad(rest, ((0, -rest.shape[0] % 16), (0, 0)))
        grad_x_t = dot(tied(N.grad_x, get(N.grad_proj)), get(N.conv_flat), ((0,), (0,)))
        grad_dt = dot(tied(N.grad_dt, get(N.rank)), get(N.grad_pre_low), ((0,), (0,)))
        return deal(grad_x_t, grad_dt, rest)

    pack_steps(plan, N.k, small_grads)
    input_grad, block_out = input_grad(), block_out()
    packed = get(N.k)
    grad_dt = packed[proj_rows : proj_rows + RANK].reshape(devices, -1, shard)
    grad_dt = grad_dt.transpose(1, 0, 2).reshape(-1, channels)
    rest = packed[proj_rows + RANK :]
    by_channel = rest[NSTATE:]
    gain_part = by_channel[taps + 3]
    grad_gain = gain_part + swapped(gain_part, TENSOR)
    grad_in = jnp.stack([get(N.A), get(N.B)], axis=1)
    return (
        block_out,
        input_grad,
        grad_gain,
        grad_in,
        by_channel[:taps],
        by_channel[taps],
        packed[:proj_rows].T,
        grad_dt,
        by_channel[taps + 1],
        rest[:NSTATE].T,
        by_channel[taps + 2],
        get(N.C).T,
    )


def solution(mesh):
    both = (TENSOR, DP)
    devices, halves = mesh.shape[DP], mesh.shape[TENSOR]

    def run(tokens, segments, cotangent, norm_gain, w_in, *others):
        trees = devices == 16 and halves == 2 and w_in.shape[0] == devices * LANES
        trees = trees and w_in.shape[2] == halves * devices * LANES
        return sharded(local if trees else local_whole)(
            tokens, segments, cotangent, norm_gain, w_in, *others
        )

    def sharded(function):
        return jax.shard_map(
            function,
            mesh=mesh,
            in_specs=(
                P(None, DP, TENSOR),
                P(None, DP),
                P(None, DP, TENSOR),
                P(DP),
                P(DP, None, TENSOR),
                P(None, both),
                P(both),
                P(both, None),
                P(DP, TENSOR),
                P(both),
                P(both, None),
                P(both),
                P(TENSOR, DP),
            ),
            out_specs=(
                P(None, DP, TENSOR),
                P(None, DP, TENSOR),
                P(DP),
                P(DP, None, TENSOR),
                P(None, both),
                P(both),
                P(both, None),
                P(DP, TENSOR),
                P(both),
                P(both, None),
                P(both),
                P(TENSOR, DP),
            ),
            check_vma=False,
        )

    return run
```
